512 devices in a mesh: lat: 32 (over y, x, core), dep: 16 (over z).
Axes of the slice: x: 4, y: 4, z: 16, core: 2. Of those that a mesh axis runs over, the one named last changes fastest.
Arguments:
- x_start: float32 [2, 4, 512, 8192], P(None, None, 'lat', 'dep'), may hold values from -6 to 6
- source: float32 [2, 4, 512, 8192], P(None, None, 'lat', 'dep'), may hold values from -6 to 6
- eps_table: float32 [2, 8], replicated, may hold values from 0.25 to 2.5
- labels: int32 [512, 8192], P('lat', 'dep'), may hold values from 0 to 7
- pml_level: int32 [2, 512, 8192], P(None, 'lat', 'dep'), may hold values from 0 to 16
Outputs:
- solution: float32 [2, 4, 512, 8192], P(None, None, 'lat', 'dep')
- residual: float32 [2, 4, 512, 8192], P(None, None, 'lat', 'dep')
The draws below stay inside these ranges and needn't reach their ends.
Inputs may be any that keep to these rules, and one draw needn't show every extreme that they name: labels name regions of eps_table. `pml_level`: level 0 is outside the absorbing layer.
All inputs are finite; a program needn't handle non-finite values.
Results may differ from the reference program's by a relative error of at most 0.009.
Values sent between devices are 32-bit elements; how exact they have to be, the bound alone decides.
No kernel may reach another device: no remote copies, remote signals or barrier semaphores. Data moves between devices by JAX's collectives and lax.ppermute only.
A program may use at most 64 MiB of HBM per device.

```python
import jax
import jax.numpy as jnp
from jax import lax

S = 4
ANGLES = 4
OUTER = 4
LABELS = 8
PML = 16
COLS = 20
NX = 512
ND = 8192


def place_ends(drawn, own_key, least, top_value):
    longest = drawn.shape.index(max(drawn.shape))
    spots = []
    for shift in (0, 1):
        where = [jax.random.randint(jax.random.fold_in(own_key, axis), (), 0, length) for axis, length in enumerate(drawn.shape)]
        where[longest] = (where[longest] + shift) % drawn.shape[longest]
        spots.append(tuple(where))
    return drawn.at[spots[0]].set(least).at[spots[1]].set(top_value)


def block_scale(stream_key, dims, pieces, smallest, largest):
    def one(axis_at, shards_of):
        steps = jax.random.uniform(jax.random.fold_in(jax.random.fold_in(stream_key, 6), axis_at), (shards_of,), jnp.float32, smallest / len(pieces), largest / len(pieces))
        return jnp.repeat(jnp.exp(steps), dims[axis_at] // shards_of).reshape((-1,) + (1,) * (len(dims) - axis_at - 1))

    gain = one(*pieces[0])
    for cut in pieces[1:]:
        gain = gain * one(*cut)
    return gain


def scatter_about(own_key, dims, width, most, pieces=(), held_as=jnp.bfloat16):
    values = jax.random.normal(own_key, dims, jnp.float32) * width
    if len(pieces) > 0:
        values = block_scale(own_key, dims, pieces, -0.22, 0.18) * values
    return jnp.clip(values, min=-most, max=most).astype(held_as)


def setup_inputs(seed: int = 0) -> dict:
    arg_keys = jax.random.split(jax.random.key(seed), 6)
    x_start = scatter_about(arg_keys[0], (2, ANGLES, NX, ND), 1.0, 6.0, ((2, 32), (3, 16)), jnp.float32)
    source = scatter_about(arg_keys[1], (2, ANGLES, NX, ND), 1.0, 6.0, ((2, 32), (3, 16)), jnp.float32)
    eps_table = jnp.clip(jax.random.uniform(arg_keys[2], (2, LABELS), jnp.float32, 0.25, 2.5), 0.25, 2.5)
    labels = place_ends(jax.random.randint(arg_keys[3], (NX, ND), 0, LABELS), jax.random.fold_in(arg_keys[3], 1), 0, LABELS - 1).astype(jnp.int32)
    pml_level = place_ends(jax.random.randint(arg_keys[4], (2, NX, ND), 0, PML + 1), jax.random.fold_in(arg_keys[4], 1), 0, PML).astype(jnp.int32)
    return {"x_start": x_start, "source": source, "eps_table": eps_table, "labels": labels, "pml_level": pml_level}


sigma_peak = 4.0
k_squared = 2.0

def complex_mul(factor, field):
    real_part = factor[0][None] * field[0] - factor[1][None] * field[1]
    imag_part = factor[0][None] * field[1] + factor[1][None] * field[0]
    return jnp.stack([real_part, imag_part])

def stretch_of(level):
    sigma = sigma_peak * (level.astype(jnp.float32) / PML) ** 2
    denom = 1.0 + sigma * sigma
    return jnp.stack([1.0 / denom, -sigma / denom])

def coefficients(labels, level_lat, level_dep, eps_table):
    onehot = (labels[None] == jnp.arange(LABELS, dtype=jnp.int32)[:, None, None]).astype(jnp.float32)
    eps_real = lax.optimization_barrier(jnp.sum(eps_table[0][:, None, None] * onehot, axis=0))
    eps_imag = lax.optimization_barrier(jnp.sum(eps_table[1][:, None, None] * onehot, axis=0))
    stretch_lat = stretch_of(level_lat)
    stretch_dep = stretch_of(level_dep)
    centre = (stretch_lat + stretch_dep) * 0.25 - k_squared / 8.0 * jnp.stack([eps_real, eps_imag])
    centre = centre.at[0].add(1.0)
    return (centre, stretch_lat, stretch_dep)

def operate(padded, factors):
    centre, stretch_lat, stretch_dep = factors
    middle = padded[:, :, 1:-1, 1:-1]
    lat_sum = padded[:, :, 2:, 1:-1] + padded[:, :, :-2, 1:-1]
    dep_sum = padded[:, :, 1:-1, 2:] + padded[:, :, 1:-1, :-2]
    return complex_mul(centre, middle) - 0.125 * (complex_mul(stretch_lat, lat_sum) + complex_mul(stretch_dep, dep_sum))

def pad_one(field):
    return jnp.pad(field, ((0, 0), (0, 0), (1, 1), (1, 1)))

def mixing_of(gram_full, angles):
    normal_matrix = gram_full[angles:, angles:]
    right_part = gram_full[angles:, :angles]
    scaling = 1.0 / jnp.sqrt(jnp.diagonal(normal_matrix))
    balanced = normal_matrix * scaling[:, None] * scaling[None, :]
    factor = jnp.linalg.cholesky(balanced)
    solved = jax.scipy.linalg.cho_solve((factor, True), right_part * scaling[:, None])
    return solved * scaling[:, None]

def reference(x_start, source, eps_table, labels, pml_level):
    factors = coefficients(labels, pml_level[0], pml_level[1], eps_table)
    residual = source - operate(pad_one(x_start), factors)
    solution = x_start
    for restart in range(OUTER):
        blocks = [residual]
        for power in range(S):
            blocks.append(operate(pad_one(blocks[-1]), factors))
        krylov = jnp.stack(blocks)
        gram_full = jnp.einsum('jcaxy,kcbxy->jakb', krylov, krylov, precision=lax.Precision.HIGHEST).reshape(COLS, COLS)
        weights = mixing_of(gram_full, ANGLES).reshape(S, ANGLES, ANGLES)
        solution = solution + jnp.einsum('jcbxy,jba->caxy', krylov[:S], weights, precision=lax.Precision.HIGHEST)
        residual = residual - jnp.einsum('jcbxy,jba->caxy', krylov[1:], weights, precision=lax.Precision.HIGHEST)
    return (solution, residual)
```

```python
import functools

import jax
import jax.numpy as jnp
from jax import lax
from jax.experimental import pallas as pl
from jax.experimental.pallas import tpu as pltpu
from jax.sharding import PartitionSpec as P

S = 4
OUTER = 4
LABELS = 8
PML = 16
ANGLES = 4

sigma_peak = 4.0
k_squared = 2.0

FUSE = 2
POWERS = S * FUSE
BLOCKS = POWERS + 1
PARTS = 2 * ANGLES
WIDTH = BLOCKS * ANGLES
ROWS = 40
SCALE = 1.5
HIGH = lax.Precision.HIGHEST
SIDE = 128
GROUP = 4
LIMIT = 56 * 1024 * 1024


def shifts_of(eps_table):
    mean = jnp.mean(eps_table, axis=1)
    centre = 1.25 - 0.25 * mean[0]
    pair = (0.25 * mean[1] + 0.12) ** 2
    return jnp.stack([centre, pair])


def dot(a, b, dims):
    return lax.dot_general(a, b, (dims, ((), ())), precision=HIGH, preferred_element_type=jnp.float32)


def iota(shape, dim):
    return lax.broadcasted_iota(jnp.int32, shape, dim)


def coefficients(labels, level_lat, level_dep, table, shift, inside):
    eps_real = jnp.zeros_like(labels)
    eps_imag = jnp.zeros_like(labels)
    for k in range(LABELS):
        here = labels == float(k)
        eps_real = jnp.where(here, table[0, k], eps_real)
        eps_imag = jnp.where(here, table[1, k], eps_imag)

    def stretch_of(level):
        sigma = sigma_peak * (level * (1.0 / PML)) ** 2
        inverse = 1.0 / (1.0 + sigma * sigma)
        return inverse, -sigma * inverse

    lat_real, lat_imag = stretch_of(level_lat)
    dep_real, dep_imag = stretch_of(level_dep)
    centre_real = (lat_real + dep_real) * 0.25 - k_squared / 8.0 * eps_real + (1.0 - shift)
    centre_imag = (lat_imag + dep_imag) * 0.25 - k_squared / 8.0 * eps_imag
    side = -0.125 * SCALE
    found = (
        SCALE * centre_real,
        side * lat_real,
        side * dep_real,
        SCALE * centre_imag,
        side * lat_imag,
        side * dep_imag,
    )
    return [jnp.where(inside, f, 0.0) for f in found]


def by_cells(fields, rows):
    return jnp.swapaxes(fields.reshape(PARTS, rows, fields.shape[1]), 0, 1)


def by_fields(cells):
    return jnp.swapaxes(cells, 0, 1).reshape(-1, cells.shape[2])


def spread_rows(compact, spread, first, count):
    sign = jnp.where(iota((PARTS, 1), 0) < ANGLES, 1.0, -1.0)

    def some(base, rows):
        for i in range(rows):
            for k in range(6):
                line = jnp.broadcast_to(compact[k, pl.ds(first + base + i, 1), :], spread.shape[2:])
                spread[k, base + i] = line * sign if k >= 3 else line

    lax.fori_loop(0, count // 8, lambda t, _: some(t * 8, 8), None)


def scaled_operator(middle, before, after, factors):
    lanes = middle.shape[1]
    lat = before + after
    dep = pltpu.roll(middle, 1, 1) + pltpu.roll(middle, lanes - 1, 1)
    straight = factors[0] * middle + factors[1] * lat + factors[2] * dep
    crossed = factors[3] * middle + factors[4] * lat + factors[5] * dep
    return straight + pltpu.roll(crossed, ANGLES, 0)


def by_groups(first, last, some):
    full = (last - first) // GROUP
    lax.fori_loop(0, full, lambda t, _: some(first + t * GROUP, GROUP), None)
    if (last - first) % GROUP:
        some(first + full * GROUP, (last - first) % GROUP)


def next_block(basis, spread, j, pair):
    rows = basis.shape[1]

    def some(base, count):
        made = []
        for i in range(count):
            x = base + i
            new = scaled_operator(
                basis[j, x], basis[j, x - 1], basis[j, x + 1], [spread[k, x] for k in range(6)]
            )
            if j % 2 == 1:
                new = new + pair * basis[j - 1, x]
            made.append(new)
        for i in range(count):
            basis[j + 1, base + i] = made[i]

    by_groups(j + 1, rows - 1 - j, some)


def packed_gram(basis, first, rows, cols):
    size = BLOCKS * PARTS

    def some(x, total):
        block = basis[:, first + x, :, 0:cols].reshape(size, cols)
        return total + dot(block, block, ((1,), (1,)))

    full = lax.fori_loop(0, rows, some, jnp.zeros((size, size), jnp.float32))
    gram = jnp.zeros((ROWS, SIDE), jnp.float32)
    for part in range(2):
        def pick(count):
            i, r = iota((count, size), 0), iota((count, size), 1)
            return jnp.where(r == (i // ANGLES) * PARTS + part * ANGLES + i % ANGLES, 1.0, 0.0)

        gram = gram + dot(dot(pick(ROWS), full, ((1,), (0,))), pick(SIDE), ((1,), (1,)))
    lane = iota((8, SIDE), 1)
    tile = jnp.zeros((8, SIDE), jnp.float32)
    for t, move in enumerate(tile_moves()):
        upper = jnp.where((lane >= 8 * t) & (lane < WIDTH), gram[8 * t : 8 * t + 8], 0.0)
        tile = tile + (pltpu.roll(upper, move, 1) if move else upper)
    return tile


def tile_moves():
    moves, at = [], 0
    for t in range(ROWS // 8):
        moves.append(at - 8 * t)
        at += WIDTH - 8 * t
    return moves


def half_gram(tile):
    lane = iota((8, SIDE), 1)
    parts = []
    for t, move in enumerate(tile_moves()):
        back = pltpu.roll(tile, SIDE - move, 1) if move else tile
        weight = jnp.where((lane >= 8 * t) & (lane < WIDTH), jnp.where(lane < 8 * t + 8, 0.5, 1.0), 0.0)
        parts.append(back * weight)
    return jnp.concatenate(parts, axis=0)


def solve_normal(gram):
    size = S * ANGLES
    work = gram[0:24]
    work = pltpu.roll(work, 24 - ANGLES, 0)[0:size]
    row, lane = iota((size, SIDE), 0), iota((size, SIDE), 1)
    diagonal = jnp.where(lane == row + ANGLES, work, 0.0)
    by_row = lax.rsqrt(jnp.sum(diagonal, axis=1, keepdims=True))
    by_lane = jnp.sum(diagonal, axis=0, keepdims=True)
    by_lane = jnp.where(
        (lane[0:1] >= ANGLES) & (lane[0:1] < ANGLES + size), lax.rsqrt(jnp.where(by_lane > 0.0, by_lane, 1.0)), 1.0
    )
    work = work * by_row * by_lane
    for k in range(size):
        column = jnp.broadcast_to(work[:, k + ANGLES : k + ANGLES + 1], (size, SIDE))
        line = work[k : k + 1] / column[k : k + 1]
        work = jnp.where(row == k, line, work - column * line)
    return jnp.where(lane < ANGLES, work * by_row, 0.0)


def cycles(tile, shift, pair):
    upper = half_gram(tile)
    row, lane = iota((ROWS, SIDE), 0), iota((ROWS, SIDE), 1)
    even = jnp.where((row // ANGLES) % 2 == 0, pair * SCALE, 0.0)
    residual = jnp.where((row == lane) & (lane < ANGLES), 1.0, 0.0)
    update = jnp.zeros((ROWS, SIDE), jnp.float32)
    blank = jnp.zeros((SIDE - ROWS, SIDE), jnp.float32)
    for cycle in range(FUSE):
        power = residual
        powers = residual
        for k in range(1, S + 1):
            power = (
                pltpu.roll(power, ANGLES, 0) * (1.0 / SCALE)
                + power * shift
                - pltpu.roll(power, ROWS - ANGLES, 0) * even
            )
            powers = powers + pltpu.roll(power, ANGLES * k, 1)
        half = dot(upper, jnp.concatenate([powers, blank], axis=0), ((1,), (0,)))
        gram = dot(powers, half, ((0,), (0,))) + dot(half, powers, ((0,), (0,)))
        mixing = solve_normal(gram)
        size = S * ANGLES
        low = jnp.concatenate([mixing, jnp.zeros((24 - size, SIDE), jnp.float32)], axis=0)
        high = pltpu.roll(pltpu.roll(low, ANGLES, 0), ANGLES, 1)
        both = jnp.concatenate([low + high, jnp.zeros((SIDE - 24, SIDE), jnp.float32)], axis=0)
        change = dot(powers, both, ((1,), (0,)))
        update = update + jnp.where(lane < ANGLES, change, 0.0)
        residual = residual - jnp.where(lane < ANGLES, pltpu.roll(change, SIDE - ANGLES, 1), 0.0)
    return update, residual


def set_weights(weights, which, table):
    row, lane = iota((ROWS, SIDE), 0), iota((ROWS, SIDE), 1)
    low = iota((8, SIDE), 0) < ANGLES
    for d in range(ANGLES):
        picked = jnp.where(lane == (row - d + ANGLES) % ANGLES, table, 0.0)
        picked = jnp.broadcast_to(jnp.sum(picked, axis=1, keepdims=True), (ROWS, SIDE))
        for j in range(BLOCKS):
            pairs = picked[8 * (j // 2) : 8 * (j // 2) + 8]
            other = pltpu.roll(pairs, ANGLES, 0)
            weights[which, d, j] = jnp.where(low, pairs, other) if j % 2 == 0 else jnp.where(low, other, pairs)


def mixed(weights, which, blocks):
    lanes = blocks[0].shape[1]
    angle = iota((PARTS, lanes), 0) % ANGLES
    total = None
    for d in range(ANGLES):
        turned = None
        for j, block in enumerate(blocks):
            factor = weights[which, d, j]
            term = jnp.concatenate([factor] * (lanes // SIDE), axis=1) * block
            turned = term if turned is None else turned + term
        if d:
            turned = jnp.where(
                angle + d < ANGLES, pltpu.roll(turned, PARTS - d, 0), pltpu.roll(turned, ANGLES - d, 0)
            )
        total = turned if total is None else total + turned
    return total


def first_kernel(
    rows, cols, edge, shift_ref, table, own, before, after, own_side, before_side, after_side, far_before, far_after,
    basis_out, compact, sums, guess, basis, spread, sems,
):
    lanes = cols + SIDE
    shift, pair = shift_ref[0], shift_ref[1]
    fields = PARTS * rows
    for p, (main, side) in enumerate(((before, before_side), (own, own_side), (after, after_side))):
        for at, ref in ((0, main), (cols, side)):
            size = ref.shape[1]
            guess[pl.ds(1 + p * rows, rows), :, at : at + size] = by_cells(ref[0:fields, :], rows)
            basis[0, pl.ds(p * rows, rows), :, at : at + size] = by_cells(ref[fields : 2 * fields, :], rows)
        row_in = (edge[p] == 0) if p != 1 else None
        for at, ref in ((0, main), (cols, side)):
            size = ref.shape[1]
            level = [ref[2 * fields + k * rows : 2 * fields + (k + 1) * rows, :] for k in range(3)]
            inside = jnp.ones((rows, size), jnp.bool_)
            if at:
                lane = iota((rows, size), 1)
                inside = jnp.where(lane < SIDE // 2, edge[3], edge[4]) == 0
            if row_in is not None:
                inside = inside & row_in
            found = coefficients(*level, table, shift, inside)
            for k in range(6):
                compact[k, p * rows : (p + 1) * rows, at : at + size] = found[k]
    nothing = jnp.zeros((PARTS, SIDE), jnp.float32)
    guess[0, :, 0:cols] = far_before[...]
    guess[0, :, cols:lanes] = nothing
    guess[3 * rows + 1, :, 0:cols] = far_after[...]
    guess[3 * rows + 1, :, cols:lanes] = nothing
    spread_rows(compact, spread, 0, 3 * rows)

    def start(base, count):
        made = []
        for i in range(count):
            x = base + i
            middle = guess[x + 1]
            applied = scaled_operator(middle, guess[x], guess[x + 2], [spread[k, x] for k in range(6)])
            made.append(basis[0, x] - applied * (1.0 / SCALE) - shift * middle)
        for i in range(count):
            basis[0, base + i] = made[i]

    by_groups(0, 3 * rows, start)
    half = rows // 2
    copies = []
    for j in range(BLOCKS):
        copies.append(
            pltpu.make_async_copy(basis.at[j, pl.ds(half, 2 * rows)], basis_out.at[j], sems.at[j])
        )
    copies[0].start()
    for j in range(POWERS):
        next_block(basis, spread, j, pair * SCALE * SCALE)
        copies[j + 1].start()
    tile = packed_gram(basis, rows, rows, cols)
    for i in range(sums.shape[0]):
        sums[i] = tile
    for copy in copies:
        copy.wait()


def second_kernel(
    rows, cols, shift_ref, tiles, basis_in, compact, start, basis_out, solution, sums, old, basis, spread, weights,
    in_sems, out_sems,
):
    shift, pair = shift_ref[0], shift_ref[1]
    fetches = [pltpu.make_async_copy(basis_in.at[j], old.at[j], in_sems.at[j]) for j in range(BLOCKS)]
    for fetch in fetches:
        fetch.start()
    half = rows // 2
    spread_rows(compact, spread, half, 2 * rows)
    update, residual = cycles(jnp.sum(tiles[...], axis=0), shift, pair)
    set_weights(weights, 0, residual)
    set_weights(weights, 1, update)
    for fetch in fetches:
        fetch.wait()

    def one(x, _):
        basis[0, x] = mixed(weights, 0, [old[j, x] for j in range(BLOCKS)])

    lax.fori_loop(0, 2 * rows, one, None)

    solution[...] = by_cells(start[...], rows)

    def move(x, _):
        solution[x] = solution[x] + mixed(weights, 1, [old[j, half + x, :, 0:cols] for j in range(POWERS)])

    lax.fori_loop(0, rows, move, None)
    copies = []
    for j in range(BLOCKS):
        copies.append(
            pltpu.make_async_copy(
                basis.at[j, pl.ds(half, rows), :, pl.ds(0, cols)], basis_out.at[j], out_sems.at[j]
            )
        )
    copies[0].start()
    for j in range(POWERS):
        next_block(basis, spread, j, pair * SCALE * SCALE)
        copies[j + 1].start()
    tile = packed_gram(basis, half, rows, cols)
    for i in range(sums.shape[0]):
        sums[i] = tile
    for copy in copies:
        copy.wait()


def third_kernel(rows, cols, shift_ref, tiles, basis_in, start, solution, residual, made, old, weights, in_sems):
    shift, pair = shift_ref[0], shift_ref[1]
    fetches = [pltpu.make_async_copy(basis_in.at[j], old.at[j], in_sems.at[j]) for j in range(BLOCKS)]
    for fetch in fetches:
        fetch.start()
    update, left = cycles(jnp.sum(tiles[...], axis=0), shift, pair)
    set_weights(weights, 0, left)
    set_weights(weights, 1, update)
    for fetch in fetches:
        fetch.wait()

    def move(x, _):
        blocks = [old[j, x] for j in range(BLOCKS)]
        made[0, x] = mixed(weights, 0, blocks)
        made[1, x] = start[x] + mixed(weights, 1, blocks[:POWERS])

    lax.fori_loop(0, rows, move, None)
    residual[...] = by_fields(made[0])
    solution[...] = by_fields(made[1])


def summed(copies):
    got = lax.all_to_all(copies, "lat", 0, 0, tiled=True)
    near = jnp.sum(got, axis=0)
    sent = jnp.broadcast_to(near[None], (lax.axis_size("dep"),) + near.shape)
    return lax.all_to_all(sent, "dep", 0, 0, tiled=True)


def shards(x_start, source, eps_table, labels, pml_level):
    rows, cols = labels.shape
    lanes = cols + SIDE
    f32 = jnp.float32
    vmem = pl.BlockSpec(memory_space=pltpu.VMEM)
    smem = pl.BlockSpec(memory_space=pltpu.SMEM)
    anywhere = pl.BlockSpec(memory_space=pl.ANY)
    params = pltpu.CompilerParams(vmem_limit_bytes=LIMIT)
    lat, dep = lax.axis_index("lat"), lax.axis_index("dep")
    lat_size, dep_size = lax.axis_size("lat"), lax.axis_size("dep")
    shift = shifts_of(eps_table)
    start = x_start.reshape(PARTS * rows, cols)
    fields = jnp.concatenate(
        [
            start,
            source.reshape(PARTS * rows, cols),
            labels.astype(f32),
            pml_level.astype(f32).reshape(2 * rows, cols),
        ]
    )

    def along(array, axis, step):
        size = lax.axis_size(axis)
        return lax.ppermute(array, axis, [(i, i + step) for i in range(size) if 0 <= i + step < size])

    before = along(fields, "lat", 1)
    after = along(fields, "lat", -1)
    right = along(fields[:, :SIDE], "dep", -1)
    left = along(fields[:, cols - SIDE :], "dep", 1)
    far_before = along(x_start[:, :, rows - 1].reshape(PARTS, cols), "lat", 2)
    far_after = along(x_start[:, :, 0].reshape(PARTS, cols), "lat", -2)
    side = jnp.where(iota(right.shape, 1) < SIDE // 2, right, left)
    before_side = along(side, "lat", 1)
    after_side = along(side, "lat", -1)
    zero = jnp.zeros((), jnp.int32)
    edge = jnp.stack(
        [
            (lat == 0).astype(jnp.int32),
            zero,
            (lat == lat_size - 1).astype(jnp.int32),
            (dep == dep_size - 1).astype(jnp.int32),
            (dep == 0).astype(jnp.int32),
        ]
    )

    basis, compact, sums = pl.pallas_call(
        functools.partial(first_kernel, rows, cols),
        out_shape=[
            jax.ShapeDtypeStruct((BLOCKS, 2 * rows, PARTS, lanes), f32),
            jax.ShapeDtypeStruct((6, 3 * rows, lanes), f32),
            jax.ShapeDtypeStruct((lat_size, 8, SIDE), f32),
        ],
        in_specs=[smem, smem, smem] + [vmem] * 8,
        out_specs=[anywhere, vmem, vmem],
        scratch_shapes=[
            pltpu.VMEM((3 * rows + 2, PARTS, lanes), f32),
            pltpu.VMEM((BLOCKS, 3 * rows, PARTS, lanes), f32),
            pltpu.VMEM((6, 3 * rows, PARTS, lanes), f32),
            pltpu.SemaphoreType.DMA((BLOCKS,)),
        ],
        compiler_params=params,
        name="first",
    )(edge, shift, eps_table, fields, before, after, side, before_side, after_side, far_before, far_after)
    tiles = summed(sums)
    basis, solution, sums = pl.pallas_call(
        functools.partial(second_kernel, rows, cols),
        out_shape=[
            jax.ShapeDtypeStruct((BLOCKS, rows, PARTS, cols), f32),
            jax.ShapeDtypeStruct((rows, PARTS, cols), f32),
            jax.ShapeDtypeStruct((lat_size, 8, SIDE), f32),
        ],
        in_specs=[smem, vmem, anywhere, vmem, vmem],
        out_specs=[anywhere, vmem, vmem],
        scratch_shapes=[
            pltpu.VMEM((BLOCKS, 2 * rows, PARTS, lanes), f32),
            pltpu.VMEM((BLOCKS, 2 * rows, PARTS, lanes), f32),
            pltpu.VMEM((6, 2 * rows, PARTS, lanes), f32),
            pltpu.VMEM((2, ANGLES, BLOCKS, 8, SIDE), f32),
            pltpu.SemaphoreType.DMA((BLOCKS,)),
            pltpu.SemaphoreType.DMA((BLOCKS,)),
        ],
        compiler_params=params,
        name="second",
    )(shift, tiles, basis, compact, start)
    tiles = summed(sums)
    solution, residual = pl.pallas_call(
        functools.partial(third_kernel, rows, cols),
        out_shape=[jax.ShapeDtypeStruct((PARTS * rows, cols), f32)] * 2,
        in_specs=[smem, vmem, anywhere, vmem],
        out_specs=[vmem, vmem],
        scratch_shapes=[
            pltpu.VMEM((2, rows, PARTS, cols), f32),
            pltpu.VMEM((BLOCKS, rows, PARTS, cols), f32),
            pltpu.VMEM((2, ANGLES, BLOCKS, 8, SIDE), f32),
            pltpu.SemaphoreType.DMA((BLOCKS,)),
        ],
        compiler_params=params,
        name="third",
    )(shift, tiles, basis, solution)
    return solution.reshape(x_start.shape), residual.reshape(x_start.shape)


def solution(mesh):
    in_specs = (
        P(None, None, "lat", "dep"),
        P(None, None, "lat", "dep"),
        P(),
        P("lat", "dep"),
        P(None, "lat", "dep"),
    )
    out_specs = (P(None, None, "lat", "dep"), P(None, None, "lat", "dep"))
    return jax.shard_map(shards, mesh=mesh, in_specs=in_specs, out_specs=out_specs, check_vma=False)
```

```python
import functools

import jax
import jax.numpy as jnp
from jax import lax
from jax.experimental import pallas as pl
from jax.experimental.pallas import tpu as pltpu
from jax.sharding import PartitionSpec as P

S = 4
OUTER = 4
LABELS = 8
PML = 16
ANGLES = 4

sigma_peak = 4.0
k_squared = 2.0

FUSE = 2
POWERS = S * FUSE
BLOCKS = POWERS + 1
PARTS = 2 * ANGLES
WIDTH = BLOCKS * ANGLES
ROWS = 40
SCALE = 1.5
HIGH = lax.Precision.HIGHEST
SIDE = 128
GROUP = 24
LIMIT = 56 * 1024 * 1024


def shifts_of(table):
    real, imag = [sum(table[part, k] for k in range(LABELS)) * (1.0 / LABELS) for part in range(2)]
    root = 0.25 * imag + 0.12
    return 1.25 - 0.25 * real, root * root


def dot(a, b, dims):
    return lax.dot_general(a, b, (dims, ((), ())), precision=HIGH, preferred_element_type=jnp.float32)


def iota(shape, dim):
    return lax.broadcasted_iota(jnp.int32, shape, dim)


def coefficients(labels, level_lat, level_dep, table, shift):
    eps_real = jnp.zeros_like(labels)
    eps_imag = jnp.zeros_like(labels)
    for k in range(LABELS):
        here = labels == float(k + 1)
        eps_real = jnp.where(here, table[0, k], eps_real)
        eps_imag = jnp.where(here, table[1, k], eps_imag)

    def stretch_of(level):
        sigma = sigma_peak * (level * (1.0 / PML)) ** 2
        inverse = 1.0 / (1.0 + sigma * sigma)
        return inverse, -sigma * inverse

    lat_real, lat_imag = stretch_of(level_lat)
    dep_real, dep_imag = stretch_of(level_dep)
    centre_real = (lat_real + dep_real) * 0.25 - k_squared / 8.0 * eps_real + (1.0 - shift)
    centre_imag = (lat_imag + dep_imag) * 0.25 - k_squared / 8.0 * eps_imag
    side = -0.125 * SCALE
    found = (
        SCALE * centre_real,
        side * lat_real,
        side * dep_real,
        SCALE * centre_imag,
        side * lat_imag,
        side * dep_imag,
    )
    return [jnp.where(labels > 0.5, f, 0.0) for f in found]


def by_cells(fields, rows):
    return jnp.swapaxes(fields.reshape(PARTS, rows, fields.shape[1]), 0, 1)


def by_fields(cells):
    return jnp.swapaxes(cells, 0, 1).reshape(-1, cells.shape[2])


def spread_rows(compact, spread, first, count):
    sign = jnp.where(iota((PARTS, 1), 0) < ANGLES, 1.0, -1.0)

    def some(base, rows):
        for i in range(rows):
            for k in range(6):
                line = jnp.broadcast_to(compact[k, pl.ds(first + base + i, 1), :], spread.shape[2:])
                spread[k, base + i] = line * sign if k >= 3 else line

    lax.fori_loop(0, count // 8, lambda t, _: some(t * 8, 8), None)


def scaled_operator(middle, before, after, factors):
    lanes = middle.shape[1]
    lat = before + after
    dep = pltpu.roll(middle, 1, 1) + pltpu.roll(middle, lanes - 1, 1)
    straight = factors[0] * middle + factors[1] * lat + factors[2] * dep
    crossed = factors[3] * middle + factors[4] * lat + factors[5] * dep
    return straight + pltpu.roll(crossed, ANGLES, 0)


def by_groups(first, last, some):
    full = (last - first) // GROUP
    lax.fori_loop(0, full, lambda t, _: some(first + t * GROUP, GROUP), None)
    if (last - first) % GROUP:
        some(first + full * GROUP, (last - first) % GROUP)


def next_block(basis, spread, j, pair):
    rows = basis.shape[1]

    def some(base, count):
        made = []
        for i in range(count):
            x = base + i
            new = scaled_operator(
                basis[j, x], basis[j, x - 1], basis[j, x + 1], [spread[k, x] for k in range(6)]
            )
            if j % 2 == 1:
                new = new + pair * basis[j - 1, x]
            made.append(new)
        for i in range(count):
            basis[j + 1, base + i] = made[i]

    by_groups(j + 1, rows - 1 - j, some)


def packed_gram(basis, first, rows, cols):
    size = BLOCKS * PARTS

    full = jnp.zeros((size, size), jnp.float32)
    for x in range(rows):
        block = basis[:, first + x, :, 0:cols].reshape(size, cols)
        full = full + dot(block, block, ((1,), (1,)))
    gram = jnp.zeros((ROWS, SIDE), jnp.float32)
    for part in range(2):
        def pick(count):
            i, r = iota((count, size), 0), iota((count, size), 1)
            return jnp.where(r == (i // ANGLES) * PARTS + part * ANGLES + i % ANGLES, 1.0, 0.0)

        gram = gram + dot(dot(pick(ROWS), full, ((1,), (0,))), pick(SIDE), ((1,), (1,)))
    lane = iota((8, SIDE), 1)
    tile = jnp.zeros((8, SIDE), jnp.float32)
    for t, move in enumerate(tile_moves()):
        upper = jnp.where((lane >= 8 * t) & (lane < WIDTH), gram[8 * t : 8 * t + 8], 0.0)
        tile = tile + (pltpu.roll(upper, move, 1) if move else upper)
    return tile


def tile_moves():
    moves, at = [], 0
    for t in range(ROWS // 8):
        moves.append(at - 8 * t)
        at += WIDTH - 8 * t
    return moves


def half_gram(tile):
    lane = iota((8, SIDE), 1)
    parts = []
    for t, move in enumerate(tile_moves()):
        back = pltpu.roll(tile, SIDE - move, 1) if move else tile
        weight = jnp.where((lane >= 8 * t) & (lane < WIDTH), jnp.where(lane < 8 * t + 8, 0.5, 1.0), 0.0)
        parts.append(back * weight)
    return jnp.concatenate(parts, axis=0)


def solve_normal(gram):
    size = S * ANGLES
    work = gram[0:24]
    work = pltpu.roll(work, 24 - ANGLES, 0)[0:size]
    row, lane = iota((size, SIDE), 0), iota((size, SIDE), 1)
    diagonal = jnp.where(lane == row + ANGLES, work, 0.0)
    by_row = lax.rsqrt(jnp.sum(diagonal, axis=1, keepdims=True))
    by_lane = jnp.sum(diagonal, axis=0, keepdims=True)
    by_lane = jnp.where(
        (lane[0:1] >= ANGLES) & (lane[0:1] < ANGLES + size), lax.rsqrt(jnp.where(by_lane > 0.0, by_lane, 1.0)), 1.0
    )
    work = work * by_row * by_lane
    for k in range(0, size, 2):
        one, two = [jnp.broadcast_to(work[:, i : i + 1], (size, SIDE)) for i in (k + ANGLES, k + ANGLES + 1)]
        upper, lower = work[k : k + 1], work[k + 1 : k + 2]
        a, b, c, d = one[k : k + 1], two[k : k + 1], one[k + 1 : k + 2], two[k + 1 : k + 2]
        inverse = 1.0 / (a * d - b * c)
        first, second = (d * upper - b * lower) * inverse, (a * lower - c * upper) * inverse
        work = jnp.where(row == k, first, jnp.where(row == k + 1, second, work - one * first - two * second))
    return jnp.where(lane < ANGLES, work * by_row, 0.0)


def cycles(tile, shift, pair):
    upper = half_gram(tile)
    row, lane = iota((ROWS, SIDE), 0), iota((ROWS, SIDE), 1)
    even = jnp.where((row // ANGLES) % 2 == 0, pair * SCALE, 0.0)
    residual = jnp.where((row == lane) & (lane < ANGLES), 1.0, 0.0)
    update = jnp.zeros((ROWS, SIDE), jnp.float32)
    blank = jnp.zeros((SIDE - ROWS, SIDE), jnp.float32)
    for cycle in range(FUSE):
        power = residual
        powers = residual
        for k in range(1, S + 1):
            power = (
                pltpu.roll(power, ANGLES, 0) * (1.0 / SCALE)
                + power * shift
                - pltpu.roll(power, ROWS - ANGLES, 0) * even
            )
            powers = powers + pltpu.roll(power, ANGLES * k, 1)
        half = dot(upper, jnp.concatenate([powers, blank], axis=0), ((1,), (0,)))
        gram = dot(powers, half, ((0,), (0,))) + dot(half, powers, ((0,), (0,)))
        mixing = solve_normal(gram)
        size = S * ANGLES
        low = jnp.concatenate([mixing, jnp.zeros((24 - size, SIDE), jnp.float32)], axis=0)
        high = pltpu.roll(pltpu.roll(low, ANGLES, 0), ANGLES, 1)
        both = jnp.concatenate([low + high, jnp.zeros((SIDE - 24, SIDE), jnp.float32)], axis=0)
        change = dot(powers, both, ((1,), (0,)))
        update = update + jnp.where(lane < ANGLES, change, 0.0)
        residual = residual - jnp.where(lane < ANGLES, pltpu.roll(change, SIDE - ANGLES, 1), 0.0)
    return update, residual


def set_weights(weights, which, table):
    row, lane = iota((ROWS, SIDE), 0), iota((ROWS, SIDE), 1)
    low = iota((8, SIDE), 0) < ANGLES
    for d in range(ANGLES):
        picked = jnp.where(lane == (row - d + ANGLES) % ANGLES, table, 0.0)
        picked = jnp.broadcast_to(jnp.sum(picked, axis=1, keepdims=True), (ROWS, SIDE))
        for j in range(BLOCKS):
            pairs = picked[8 * (j // 2) : 8 * (j // 2) + 8]
            other = pltpu.roll(pairs, ANGLES, 0)
            weights[which, d, j] = jnp.where(low, pairs, other) if j % 2 == 0 else jnp.where(low, other, pairs)


def mixed(weights, which, blocks):
    lanes = blocks[0].shape[1]
    angle = iota((PARTS, lanes), 0) % ANGLES
    total = None
    for d in range(ANGLES):
        turned = None
        for j, block in enumerate(blocks):
            factor = weights[which, d, j]
            term = jnp.concatenate([factor] * (lanes // SIDE), axis=1) * block
            turned = term if turned is None else turned + term
        if d:
            turned = jnp.where(
                angle + d < ANGLES, pltpu.roll(turned, PARTS - d, 0), pltpu.roll(turned, ANGLES - d, 0)
            )
        total = turned if total is None else total + turned
    return total


def pack_kernel(rows, cols, start, source, labels, levels, fields, first, last):
    size = PARTS * rows
    for at, value in (
        (0, start[...]),
        (size, source[...]),
        (2 * size, (labels[...] + 1).astype(jnp.float32)),
        (2 * size + rows, levels[...].astype(jnp.float32)),
    ):
        here = slice(at, at + value.shape[0])
        fields[here, :] = value
        first[here, :] = value[:, 0:SIDE]
        last[here, :] = value[:, cols - SIDE : cols]


def side_kernel(rows, cols, right, left, before, after, up, down):
    size = right.shape[0]
    side = jnp.where(iota(right.shape, 1) < SIDE // 2, right[...], left[...])
    for out, ref, row in ((up, before, rows - 1), (down, after, 0)):
        out[0:size, :] = side
        far = jnp.concatenate([ref[f * rows + row : f * rows + row + 1, :] for f in range(PARTS)], axis=0)
        for t in range(cols // SIDE):
            out[size + t * PARTS : size + (t + 1) * PARTS, :] = far[:, t * SIDE : (t + 1) * SIDE]


def first_kernel(
    rows, cols, table, own, before, after, own_side, before_side, after_side, basis_out, compact, sums, guess, basis,
    spread, sems,
):
    lanes = cols + SIDE
    shift, pair = shifts_of(table)
    fields = PARTS * rows
    for p, (main, side) in enumerate(((before, before_side), (own, own_side), (after, after_side))):
        for at, ref in ((0, main), (cols, side)):
            size = ref.shape[1]
            guess[pl.ds(1 + p * rows, rows), :, at : at + size] = by_cells(ref[0:fields, :], rows)
            basis[0, pl.ds(p * rows, rows), :, at : at + size] = by_cells(ref[fields : 2 * fields, :], rows)
            level = [ref[2 * fields + k * rows : 2 * fields + (k + 1) * rows, :] for k in range(3)]
            found = coefficients(*level, table, shift)
            for k in range(6):
                compact[k, p * rows : (p + 1) * rows, at : at + size] = found[k]
    end = 2 * fields + 3 * rows
    for x, ref in ((0, before_side), (3 * rows + 1, after_side)):
        for t in range(cols // SIDE):
            guess[x, :, t * SIDE : (t + 1) * SIDE] = ref[end + t * PARTS : end + (t + 1) * PARTS, :]
        guess[x, :, cols:lanes] = jnp.zeros((PARTS, SIDE), jnp.float32)
    spread_rows(compact, spread, 0, 3 * rows)

    def start(base, count):
        made = []
        for i in range(count):
            x = base + i
            middle = guess[x + 1]
            applied = scaled_operator(middle, guess[x], guess[x + 2], [spread[k, x] for k in range(6)])
            made.append(basis[0, x] - applied * (1.0 / SCALE) - shift * middle)
        for i in range(count):
            basis[0, base + i] = made[i]

    by_groups(0, 3 * rows, start)
    half = rows // 2
    copies = []
    for j in range(BLOCKS):
        copies.append(
            pltpu.make_async_copy(basis.at[j, pl.ds(half, 2 * rows)], basis_out.at[j], sems.at[j])
        )
    copies[0].start()
    for j in range(POWERS):
        next_block(basis, spread, j, pair * SCALE * SCALE)
        copies[j + 1].start()
    tile = packed_gram(basis, rows, rows, cols)
    for i in range(sums.shape[0]):
        sums[i] = tile
    for copy in copies:
        copy.wait()


def second_kernel(
    rows, cols, table, tiles, basis_in, compact, start, basis_out, solution, sums, old, basis, spread, weights,
    in_sems, out_sems,
):
    shift, pair = shifts_of(table)
    fetches = [pltpu.make_async_copy(basis_in.at[j], old.at[j], in_sems.at[j]) for j in range(BLOCKS)]
    for fetch in fetches:
        fetch.start()
    half = rows // 2
    spread_rows(compact, spread, half, 2 * rows)
    update, residual = cycles(jnp.sum(tiles[...], axis=0), shift, pair)
    set_weights(weights, 0, residual)
    set_weights(weights, 1, update)
    for fetch in fetches:
        fetch.wait()

    def one(x, _):
        basis[0, x] = mixed(weights, 0, [old[j, x] for j in range(BLOCKS)])

    lax.fori_loop(0, 2 * rows, one, None)

    solution[...] = by_cells(start[...], rows)

    def move(x, _):
        solution[x] = solution[x] + mixed(weights, 1, [old[j, half + x, :, 0:cols] for j in range(POWERS)])

    lax.fori_loop(0, rows, move, None)
    copies = []
    for j in range(BLOCKS):
        copies.append(
            pltpu.make_async_copy(
                basis.at[j, pl.ds(half, rows), :, pl.ds(0, cols)], basis_out.at[j], out_sems.at[j]
            )
        )
    copies[0].start()
    for j in range(POWERS):
        next_block(basis, spread, j, pair * SCALE * SCALE)
        copies[j + 1].start()
    tile = packed_gram(basis, half, rows, cols)
    for i in range(sums.shape[0]):
        sums[i] = tile
    for copy in copies:
        copy.wait()


def third_kernel(rows, cols, table, tiles, basis_in, start, solution, residual, made, old, weights, in_sems):
    shift, pair = shifts_of(table)
    fetches = [pltpu.make_async_copy(basis_in.at[j], old.at[j], in_sems.at[j]) for j in range(BLOCKS)]
    for fetch in fetches:
        fetch.start()
    update, left = cycles(jnp.sum(tiles[...], axis=0), shift, pair)
    set_weights(weights, 0, left)
    set_weights(weights, 1, update)
    for fetch in fetches:
        fetch.wait()

    def move(x, _):
        blocks = [old[j, x] for j in range(BLOCKS)]
        made[0, x] = mixed(weights, 0, blocks)
        made[1, x] = start[x] + mixed(weights, 1, blocks[:POWERS])

    lax.fori_loop(0, rows, move, None)
    residual[...] = by_fields(made[0])
    solution[...] = by_fields(made[1])


def summed(copies):
    got = lax.all_to_all(copies, "lat", 0, 0, tiled=True)
    near = jnp.sum(got, axis=0)
    sent = jnp.broadcast_to(near[None], (lax.axis_size("dep"),) + near.shape)
    return lax.all_to_all(sent, "dep", 0, 0, tiled=True)


def shards(x_start, source, eps_table, labels, pml_level):
    rows, cols = labels.shape
    lanes = cols + SIDE
    f32 = jnp.float32
    vmem = pl.BlockSpec(memory_space=pltpu.VMEM)
    smem = pl.BlockSpec(memory_space=pltpu.SMEM)
    anywhere = pl.BlockSpec(memory_space=pl.ANY)
    params = pltpu.CompilerParams(vmem_limit_bytes=LIMIT)
    lat_size = lax.axis_size("lat")
    start = x_start.reshape(PARTS * rows, cols)
    height = (2 * PARTS + 3) * rows
    fields, first, last = pl.pallas_call(
        functools.partial(pack_kernel, rows, cols),
        out_shape=[jax.ShapeDtypeStruct((height, size), f32) for size in (cols, SIDE, SIDE)],
        in_specs=[vmem] * 4,
        out_specs=[vmem] * 3,
        compiler_params=params,
        name="pack",
    )(start, source.reshape(PARTS * rows, cols), labels, pml_level.reshape(2 * rows, cols))

    def along(array, axis, step):
        size = lax.axis_size(axis)
        return lax.ppermute(array, axis, [(i, i + step) for i in range(size) if 0 <= i + step < size])

    before, after = along(fields, "lat", 1), along(fields, "lat", -1)
    right, left = along(first, "dep", -1), along(last, "dep", 1)
    guesses = pl.BlockSpec((PARTS * rows, cols), lambda i: (0, 0))
    whole = pl.BlockSpec((height, SIDE), lambda i: (0, 0))
    tall = height + cols // SIDE * PARTS
    up, down = pl.pallas_call(
        functools.partial(side_kernel, rows, cols),
        grid=(1,),
        out_shape=[jax.ShapeDtypeStruct((tall, SIDE), f32)] * 2,
        in_specs=[whole, whole, guesses, guesses],
        out_specs=[pl.BlockSpec((tall, SIDE), lambda i: (0, 0))] * 2,
        compiler_params=params,
        name="side",
    )(right, left, before, after)
    before_side, after_side = along(up, "lat", 1), along(down, "lat", -1)

    basis, compact, sums = pl.pallas_call(
        functools.partial(first_kernel, rows, cols),
        out_shape=[
            jax.ShapeDtypeStruct((BLOCKS, 2 * rows, PARTS, lanes), f32),
            jax.ShapeDtypeStruct((6, 3 * rows, lanes), f32),
            jax.ShapeDtypeStruct((lat_size, 8, SIDE), f32),
        ],
        in_specs=[smem] + [vmem] * 6,
        out_specs=[anywhere, vmem, vmem],
        scratch_shapes=[
            pltpu.VMEM((3 * rows + 2, PARTS, lanes), f32),
            pltpu.VMEM((BLOCKS, 3 * rows, PARTS, lanes), f32),
            pltpu.VMEM((6, 3 * rows, PARTS, lanes), f32),
            pltpu.SemaphoreType.DMA((BLOCKS,)),
        ],
        compiler_params=params,
        name="first",
    )(eps_table, fields, before, after, up, before_side, after_side)
    tiles = summed(sums)
    basis, solution, sums = pl.pallas_call(
        functools.partial(second_kernel, rows, cols),
        out_shape=[
            jax.ShapeDtypeStruct((BLOCKS, rows, PARTS, cols), f32),
            jax.ShapeDtypeStruct((rows, PARTS, cols), f32),
            jax.ShapeDtypeStruct((lat_size, 8, SIDE), f32),
        ],
        in_specs=[smem, vmem, anywhere, vmem, vmem],
        out_specs=[anywhere, vmem, vmem],
        scratch_shapes=[
            pltpu.VMEM((BLOCKS, 2 * rows, PARTS, lanes), f32),
            pltpu.VMEM((BLOCKS, 2 * rows, PARTS, lanes), f32),
            pltpu.VMEM((6, 2 * rows, PARTS, lanes), f32),
            pltpu.VMEM((2, ANGLES, BLOCKS, 8, SIDE), f32),
            pltpu.SemaphoreType.DMA((BLOCKS,)),
            pltpu.SemaphoreType.DMA((BLOCKS,)),
        ],
        compiler_params=params,
        name="second",
    )(eps_table, tiles, basis, compact, start)
    tiles = summed(sums)
    solution, residual = pl.pallas_call(
        functools.partial(third_kernel, rows, cols),
        out_shape=[jax.ShapeDtypeStruct((PARTS * rows, cols), f32)] * 2,
        in_specs=[smem, vmem, anywhere, vmem],
        out_specs=[vmem, vmem],
        scratch_shapes=[
            pltpu.VMEM((2, rows, PARTS, cols), f32),
            pltpu.VMEM((BLOCKS, rows, PARTS, cols), f32),
            pltpu.VMEM((2, ANGLES, BLOCKS, 8, SIDE), f32),
            pltpu.SemaphoreType.DMA((BLOCKS,)),
        ],
        compiler_params=params,
        name="third",
    )(eps_table, tiles, basis, solution)
    return solution.reshape(x_start.shape), residual.reshape(x_start.shape)


def solution(mesh):
    in_specs = (
        P(None, None, "lat", "dep"),
        P(None, None, "lat", "dep"),
        P(),
        P("lat", "dep"),
        P(None, "lat", "dep"),
    )
    out_specs = (P(None, None, "lat", "dep"), P(None, None, "lat", "dep"))
    return jax.shard_map(shards, mesh=mesh, in_specs=in_specs, out_specs=out_specs, check_vma=False)
```

```python
import functools

import jax
import jax.numpy as jnp
from jax import lax
from jax.experimental import pallas as pl
from jax.experimental.pallas import tpu as pltpu
from jax.sharding import PartitionSpec as P

S = 4
OUTER = 4
LABELS = 8
PML = 16
ANGLES = 4

sigma_peak = 4.0
k_squared = 2.0

FUSE = 2
POWERS = S * FUSE
BLOCKS = POWERS + 1
PARTS = 2 * ANGLES
HEIGHT = BLOCKS * PARTS
SCALE = 1.5
HIGH = lax.Precision.HIGHEST
SIDE = 128
GROUP = 24
LIMIT = 56 * 1024 * 1024


def shifts_of(table):
    real, imag = [sum(table[part, k] for k in range(LABELS)) * (1.0 / LABELS) for part in range(2)]
    root = 0.25 * imag + 0.12
    return 1.25 - 0.25 * real, root * root


def dot(a, b, dims):
    return lax.dot_general(a, b, (dims, ((), ())), precision=HIGH, preferred_element_type=jnp.float32)


def iota(shape, dim):
    return lax.broadcasted_iota(jnp.int32, shape, dim)


def coefficients(labels, level_lat, level_dep, table, shift):
    eps_real = jnp.zeros_like(labels)
    eps_imag = jnp.zeros_like(labels)
    for k in range(LABELS):
        here = labels == float(k + 1)
        eps_real = jnp.where(here, table[0, k], eps_real)
        eps_imag = jnp.where(here, table[1, k], eps_imag)

    def stretch_of(level):
        sigma = sigma_peak * (level * (1.0 / PML)) ** 2
        inverse = 1.0 / (1.0 + sigma * sigma)
        return inverse, -sigma * inverse

    lat_real, lat_imag = stretch_of(level_lat)
    dep_real, dep_imag = stretch_of(level_dep)
    centre_real = (lat_real + dep_real) * 0.25 - k_squared / 8.0 * eps_real + (1.0 - shift)
    centre_imag = (lat_imag + dep_imag) * 0.25 - k_squared / 8.0 * eps_imag
    side = -0.125 * SCALE
    found = (
        SCALE * centre_real,
        side * lat_real,
        side * dep_real,
        SCALE * centre_imag,
        side * lat_imag,
        side * dep_imag,
    )
    return [jnp.where(labels > 0.5, f, 0.0) for f in found]


def by_cells(fields, rows):
    return jnp.swapaxes(fields.reshape(PARTS, rows, fields.shape[1]), 0, 1)


def by_fields(cells):
    return jnp.swapaxes(cells, 0, 1).reshape(-1, cells.shape[2])


def spread_rows(compact, spread, first, count):
    sign = jnp.where(iota((PARTS, 1), 0) < ANGLES, 1.0, -1.0)

    for x in range(first, first + count):
        for k in range(6):
            line = jnp.broadcast_to(compact[k, x : x + 1, :], spread.shape[2:])
            spread[k, x] = line * sign if k >= 3 else line


def scaled_operator(middle, before, after, factors):
    lanes = middle.shape[1]
    lat = before + after
    dep = pltpu.roll(middle, 1, 1) + pltpu.roll(middle, lanes - 1, 1)
    straight = factors[0] * middle + factors[1] * lat + factors[2] * dep
    crossed = factors[3] * middle + factors[4] * lat + factors[5] * dep
    return straight + pltpu.roll(crossed, ANGLES, 0)


def by_groups(first, last, some):
    full = (last - first) // GROUP
    lax.fori_loop(0, full, lambda t, _: some(first + t * GROUP, GROUP), None)
    if (last - first) % GROUP:
        some(first + full * GROUP, (last - first) % GROUP)


def next_block(basis, spread, j, pair):
    rows = basis.shape[1]

    def some(base, count):
        made = []
        for i in range(count):
            x = base + i
            new = scaled_operator(
                basis[j, x], basis[j, x - 1], basis[j, x + 1], [spread[k, x] for k in range(6)]
            )
            if j % 2 == 1:
                new = new + pair * basis[j - 1, x]
            made.append(new)
        for i in range(count):
            basis[j + 1, base + i] = made[i]

    by_groups(j + 1, rows - 1 - j, some)


def packed_gram(basis, first, rows, cols):
    full = jnp.zeros((HEIGHT, HEIGHT), jnp.float32)
    for x in range(rows):
        block = basis[:, first + x, :, 0:cols].reshape(HEIGHT, cols)
        full = full + dot(block, block, ((1,), (1,)))
    full = jnp.concatenate([full, jnp.zeros((HEIGHT, SIDE - HEIGHT), jnp.float32)], axis=1)
    both = full + pltpu.roll(pltpu.roll(full, SIDE - ANGLES, 1), HEIGHT - ANGLES, 0)
    tile = jnp.zeros((PARTS, SIDE), jnp.float32)
    for j in range(BLOCKS):
        low, move = PLACES[j]
        upper = jnp.where(upper_lanes(j), both[PARTS * j : PARTS * (j + 1)], 0.0)
        upper = pltpu.roll(upper, move % SIDE, 1) if move else upper
        tile = tile + (pltpu.roll(upper, ANGLES, 0) if low else upper)
    return tile


PLACES = {
    0: (False, 0),
    3: (False, 72 - 24),
    8: (False, 120 - 64),
    1: (False, 0 - 8 + ANGLES),
    2: (False, 64 - 16 + ANGLES),
    4: (True, 0 - 32),
    5: (True, 40 - 40),
    6: (True, 72 - 48),
    7: (True, 96 - 56),
}


def upper_lanes(j):
    row, lane = iota((PARTS, SIDE), 0), iota((PARTS, SIDE), 1)
    return (row < ANGLES) & (lane % PARTS < ANGLES) & (lane >= PARTS * j) & (lane < HEIGHT)


def half_gram(tile):
    lane = iota((PARTS, SIDE), 1)
    parts = []
    for j in range(BLOCKS):
        low, move = PLACES[j]
        back = pltpu.roll(tile, ANGLES, 0) if low else tile
        back = pltpu.roll(back, -move % SIDE, 1) if move else back
        weight = jnp.where(lane < PARTS * (j + 1), 0.5, 1.0)
        parts.append(jnp.where(upper_lanes(j), back * weight, 0.0))
    return jnp.concatenate(parts, axis=0)


def solve_normal(gram):
    size = S * ANGLES
    work = gram[0:24]
    work = pltpu.roll(work, 24 - ANGLES, 0)[0:size]
    row, lane = iota((size, SIDE), 0), iota((size, SIDE), 1)
    diagonal = jnp.where(lane == row + ANGLES, work, 0.0)
    by_row = lax.rsqrt(jnp.sum(diagonal, axis=1, keepdims=True))
    by_lane = jnp.sum(diagonal, axis=0, keepdims=True)
    by_lane = jnp.where(
        (lane[0:1] >= ANGLES) & (lane[0:1] < ANGLES + size), lax.rsqrt(jnp.where(by_lane > 0.0, by_lane, 1.0)), 1.0
    )
    work = work * by_row * by_lane
    left = [jnp.broadcast_to(work[:, i : i + 1], (size, SIDE)) for i in range(ANGLES, ANGLES + size)] + [work]
    for k in range(0, size, 2):
        one, two = left[0], left[1]
        a, b, c, d = one[k : k + 1], two[k : k + 1], one[k + 1 : k + 2], two[k + 1 : k + 2]
        inverse = 1.0 / (a * d - b * c)
        a, b, c, d = a * inverse, b * inverse, c * inverse, d * inverse
        one, two = one - jnp.where(row == k, 1.0, 0.0), two - jnp.where(row == k + 1, 1.0, 0.0)
        after = []
        for column in left[2:]:
            upper, lower = column[k : k + 1], column[k + 1 : k + 2]
            after.append(column - one * (d * upper - b * lower) - two * (a * lower - c * upper))
        left = after
    return jnp.where(lane < ANGLES, left[0] * by_row, 0.0)


def cycles(tile, shift, pair):
    upper = half_gram(tile)
    row, lane = iota((HEIGHT, SIDE), 0), iota((HEIGHT, SIDE), 1)
    even = jnp.where(((row // PARTS) % 2 == 0) & (row < HEIGHT - PARTS), pair * SCALE, 0.0)
    residual = jnp.where((row == lane) & (lane < ANGLES), 1.0, 0.0)
    update = jnp.zeros((HEIGHT, SIDE), jnp.float32)
    blank = jnp.zeros((SIDE - HEIGHT, SIDE), jnp.float32)
    for cycle in range(FUSE):
        power = residual
        powers = residual
        for k in range(1, S + 1):
            power = (
                pltpu.roll(power, PARTS, 0) * (1.0 / SCALE)
                + power * shift
                - pltpu.roll(power, HEIGHT - PARTS, 0) * even
            )
            powers = powers + pltpu.roll(power, ANGLES * k, 1)
        half = dot(upper, jnp.concatenate([powers, blank], axis=0), ((1,), (0,)))
        gram = dot(powers, half, ((0,), (0,))) + dot(half, powers, ((0,), (0,)))
        mixing = solve_normal(gram)
        size = S * ANGLES
        low = jnp.concatenate([mixing, jnp.zeros((24 - size, SIDE), jnp.float32)], axis=0)
        high = pltpu.roll(pltpu.roll(low, ANGLES, 0), ANGLES, 1)
        both = jnp.concatenate([low + high, jnp.zeros((SIDE - 24, SIDE), jnp.float32)], axis=0)
        change = dot(powers, both, ((1,), (0,)))
        update = update + jnp.where(lane < ANGLES, change, 0.0)
        residual = residual - jnp.where(lane < ANGLES, pltpu.roll(change, SIDE - ANGLES, 1), 0.0)
    return update, residual


def set_weights(weights, which, table):
    row, lane = iota((HEIGHT, SIDE), 0), iota((HEIGHT, SIDE), 1)
    for d in range(ANGLES):
        picked = jnp.where(lane == (row - d + ANGLES) % ANGLES, table, 0.0)
        picked = jnp.broadcast_to(jnp.sum(picked, axis=1, keepdims=True), (HEIGHT, SIDE))
        for j in range(BLOCKS):
            single = picked[PARTS * j : PARTS * (j + 1)]
            weights[which, d, j] = single + pltpu.roll(single, ANGLES, 0)


def mixed(weights, which, blocks):
    lanes = blocks[0].shape[1]
    angle = iota((PARTS, lanes), 0) % ANGLES
    total = None
    for d in range(ANGLES):
        turned = None
        for j, block in enumerate(blocks):
            factor = weights[which, d, j]
            term = jnp.concatenate([factor] * (lanes // SIDE), axis=1) * block
            turned = term if turned is None else turned + term
        if d:
            turned = jnp.where(
                angle + d < ANGLES, pltpu.roll(turned, PARTS - d, 0), pltpu.roll(turned, ANGLES - d, 0)
            )
        total = turned if total is None else total + turned
    return total


def fetch(source, target, sem):
    copy = pltpu.make_async_copy(source, target, sem)
    copy.start()
    return copy


def pack_kernel(rows, cols, start, source, labels, levels, fields, first, last, marks, sems):
    size = PARTS * rows
    count = 3 * rows
    right = cols - SIDE
    copies = []
    for at, ref in ((0, start), (size, source)):
        copies.append(fetch(ref, fields.at[pl.ds(at, size)], sems.at[len(copies)]))
        copies.append(fetch(ref.at[:, pl.ds(0, SIDE)], first.at[pl.ds(at, size)], sems.at[len(copies)]))
        copies.append(fetch(ref.at[:, pl.ds(right, SIDE)], last.at[pl.ds(at, size)], sems.at[len(copies)]))
    marks[0:rows, :] = (labels[...] + 1).astype(jnp.float32)
    marks[rows:count, :] = levels[...].astype(jnp.float32)
    copies.append(fetch(marks, fields.at[pl.ds(2 * size, count)], sems.at[6]))
    copies.append(fetch(marks.at[:, pl.ds(0, SIDE)], first.at[pl.ds(2 * size, count)], sems.at[7]))
    copies.append(fetch(marks.at[:, pl.ds(right, SIDE)], last.at[pl.ds(2 * size, count)], sems.at[8]))
    for copy in copies:
        copy.wait()


def side_kernel(rows, cols, right, left, before, after, up, down, ends, sides, sems):
    size = right.shape[0]
    copies = [fetch(right, sides.at[0], sems.at[0]), fetch(left, sides.at[1], sems.at[1])]
    for f in range(PARTS):
        copies.append(fetch(before.at[pl.ds((f + 1) * rows - 8, 8)], ends.at[0, f], sems.at[2 + f]))
        copies.append(fetch(after.at[pl.ds(f * rows, 8)], ends.at[1, f], sems.at[2 + PARTS + f]))
    for copy in copies[:2]:
        copy.wait()
    side = jnp.where(iota((size, SIDE), 1) < SIDE // 2, sides[0], sides[1])
    up[0:size, :] = side
    down[0:size, :] = side
    for copy in copies[2:]:
        copy.wait()
    for out, p, row in ((up, 0, 7), (down, 1, 0)):
        far = jnp.concatenate([ends[p, f, row : row + 1, :] for f in range(PARTS)], axis=0)
        for t in range(cols // SIDE):
            out[size + t * PARTS : size + (t + 1) * PARTS, :] = far[:, t * SIDE : (t + 1) * SIDE]


def first_kernel(
    rows, cols, table, own, before, after, own_side, before_side, after_side, basis_out, spread_out, guess_out, sums,
    mains, sides, guess, basis, compact, spread, in_sems, out_sems,
):
    lanes = cols + SIDE
    shift, pair = shifts_of(table)
    fields = PARTS * rows
    parts = ((1, own, own_side), (0, before, before_side), (2, after, after_side))
    copies = {}
    for p, main, side in parts:
        copies[p] = [fetch(main, mains.at[p], in_sems.at[p]), fetch(side, sides.at[p], in_sems.at[3 + p])]
    for p, _, _ in parts:
        for copy in copies[p]:
            copy.wait()
        for at, ref in ((0, mains.at[p]), (cols, sides.at[p])):
            size = ref.shape[1]
            guess[pl.ds(1 + p * rows, rows), :, at : at + size] = by_cells(ref[0:fields, :], rows)
            basis[0, pl.ds(p * rows, rows), :, at : at + size] = by_cells(ref[fields : 2 * fields, :], rows)
            level = [ref[2 * fields + k * rows : 2 * fields + (k + 1) * rows, :] for k in range(3)]
            found = coefficients(*level, table, shift)
            for k in range(6):
                compact[k, p * rows : (p + 1) * rows, at : at + size] = found[k]
        spread_rows(compact, spread, p * rows, rows)
    end = 2 * fields + 3 * rows
    for x, p in ((0, 0), (3 * rows + 1, 2)):
        for t in range(cols // SIDE):
            guess[x, :, t * SIDE : (t + 1) * SIDE] = sides[p, end + t * PARTS : end + (t + 1) * PARTS, :]
        guess[x, :, cols:lanes] = jnp.zeros((PARTS, SIDE), jnp.float32)
    half = rows // 2
    outs = [fetch(guess.at[pl.ds(rows + 1, rows), :, pl.ds(0, cols)], guess_out, out_sems.at[BLOCKS])]
    outs.append(fetch(spread.at[:, pl.ds(half, 2 * rows)], spread_out, out_sems.at[BLOCKS + 1]))

    def start(base, count):
        made = []
        for i in range(count):
            x = base + i
            middle = guess[x + 1]
            applied = scaled_operator(middle, guess[x], guess[x + 2], [spread[k, x] for k in range(6)])
            made.append(basis[0, x] - applied * (1.0 / SCALE) - shift * middle)
        for i in range(count):
            basis[0, base + i] = made[i]

    by_groups(0, 3 * rows, start)
    outs.append(fetch(basis.at[0, pl.ds(half, 2 * rows)], basis_out.at[0], out_sems.at[0]))
    for j in range(POWERS):
        next_block(basis, spread, j, pair * SCALE * SCALE)
        outs.append(fetch(basis.at[j + 1, pl.ds(half, 2 * rows)], basis_out.at[j + 1], out_sems.at[j + 1]))
    tile = packed_gram(basis, rows, rows, cols)
    for i in range(sums.shape[0]):
        sums[i] = tile
    for copy in outs:
        copy.wait()


def second_kernel(
    rows, cols, table, tiles, basis_in, spread_in, guess_in, basis_out, solution_out, sums, old, basis, spread, guess,
    weights, in_sems, out_sems,
):
    shift, pair = shifts_of(table)
    copies = [fetch(basis_in.at[j], old.at[j], in_sems.at[j]) for j in range(BLOCKS)]
    copies.append(fetch(guess_in, guess, in_sems.at[BLOCKS]))
    copies.append(fetch(spread_in, spread, in_sems.at[BLOCKS + 1]))
    half = rows // 2
    update, residual = cycles(jnp.sum(tiles[...], axis=0), shift, pair)
    set_weights(weights, 0, residual)
    set_weights(weights, 1, update)
    for copy in copies:
        copy.wait()

    def one(t, _):
        for i in range(4):
            x = 4 * t + i
            basis[0, x] = mixed(weights, 0, [old[j, x] for j in range(BLOCKS)])

    lax.fori_loop(0, 2 * rows // 4, one, None)

    def move(t, _):
        for i in range(4):
            x = 4 * t + i
            guess[x] = guess[x] + mixed(weights, 1, [old[j, half + x, :, 0:cols] for j in range(POWERS)])

    lax.fori_loop(0, rows // 4, move, None)
    outs = [fetch(guess, solution_out, out_sems.at[BLOCKS])]
    inside = (pl.ds(half, rows), slice(None), pl.ds(0, cols))
    outs.append(fetch(basis.at[(0, *inside)], basis_out.at[0], out_sems.at[0]))
    for j in range(POWERS):
        next_block(basis, spread, j, pair * SCALE * SCALE)
        outs.append(fetch(basis.at[(j + 1, *inside)], basis_out.at[j + 1], out_sems.at[j + 1]))
    tile = packed_gram(basis, half, rows, cols)
    for i in range(sums.shape[0]):
        sums[i] = tile
    for copy in outs:
        copy.wait()


def third_kernel(rows, cols, table, tiles, basis_in, start_in, solution, residual, made, old, weights, in_sems):
    shift, pair = shifts_of(table)
    copies = [fetch(basis_in.at[j], old.at[j], in_sems.at[j]) for j in range(BLOCKS)]
    copies.append(fetch(start_in, made.at[1], in_sems.at[BLOCKS]))
    update, left = cycles(jnp.sum(tiles[...], axis=0), shift, pair)
    set_weights(weights, 0, left)
    set_weights(weights, 1, update)
    for copy in copies:
        copy.wait()

    def move(t, _):
        for i in range(4):
            x = 4 * t + i
            blocks = [old[j, x] for j in range(BLOCKS)]
            made[0, x] = mixed(weights, 0, blocks)
            made[1, x] = made[1, x] + mixed(weights, 1, blocks[:POWERS])

    lax.fori_loop(0, rows // 4, move, None)
    residual[...] = by_fields(made[0])
    solution[...] = by_fields(made[1])


def summed(copies):
    got = lax.all_to_all(copies, "lat", 0, 0, tiled=True)
    near = jnp.sum(got, axis=0)
    sent = jnp.broadcast_to(near[None], (lax.axis_size("dep"),) + near.shape)
    return lax.all_to_all(sent, "dep", 0, 0, tiled=True)


def shards(x_start, source, eps_table, labels, pml_level):
    rows, cols = labels.shape
    lanes = cols + SIDE
    f32 = jnp.float32
    vmem = pl.BlockSpec(memory_space=pltpu.VMEM)
    smem = pl.BlockSpec(memory_space=pltpu.SMEM)
    anywhere = pl.BlockSpec(memory_space=pl.ANY)
    params = pltpu.CompilerParams(vmem_limit_bytes=LIMIT)
    lat_size = lax.axis_size("lat")
    start = x_start.reshape(PARTS * rows, cols)
    height = (2 * PARTS + 3) * rows
    count = PARTS * rows
    dma = pltpu.SemaphoreType.DMA
    fields, first, last = pl.pallas_call(
        functools.partial(pack_kernel, rows, cols),
        out_shape=[jax.ShapeDtypeStruct((height, size), f32) for size in (cols, SIDE, SIDE)],
        in_specs=[anywhere, anywhere, vmem, vmem],
        out_specs=[anywhere] * 3,
        scratch_shapes=[pltpu.VMEM((3 * rows, cols), f32), dma((9,))],
        compiler_params=params,
        name="pack",
    )(start, source.reshape(count, cols), labels, pml_level.reshape(2 * rows, cols))

    def along(array, axis, step):
        size = lax.axis_size(axis)
        return lax.ppermute(array, axis, [(i, i + step) for i in range(size) if 0 <= i + step < size])

    before, after = along(fields, "lat", 1), along(fields, "lat", -1)
    right, left = along(first, "dep", -1), along(last, "dep", 1)
    tall = height + cols // SIDE * PARTS
    up, down = pl.pallas_call(
        functools.partial(side_kernel, rows, cols),
        out_shape=[jax.ShapeDtypeStruct((tall, SIDE), f32)] * 2,
        in_specs=[anywhere] * 4,
        out_specs=[vmem] * 2,
        scratch_shapes=[pltpu.VMEM((2, PARTS, 8, cols), f32), pltpu.VMEM((2, height, SIDE), f32), dma((2 + 2 * PARTS,))],
        compiler_params=params,
        name="side",
    )(right, left, before, after)
    before_side, after_side = along(up, "lat", 1), along(down, "lat", -1)

    basis, spread, guess, sums = pl.pallas_call(
        functools.partial(first_kernel, rows, cols),
        out_shape=[
            jax.ShapeDtypeStruct((BLOCKS, 2 * rows, PARTS, lanes), f32),
            jax.ShapeDtypeStruct((6, 2 * rows, PARTS, lanes), f32),
            jax.ShapeDtypeStruct((rows, PARTS, cols), f32),
            jax.ShapeDtypeStruct((lat_size, PARTS, SIDE), f32),
        ],
        in_specs=[smem] + [anywhere] * 6,
        out_specs=[anywhere] * 3 + [vmem],
        scratch_shapes=[
            pltpu.VMEM((3, height, cols), f32),
            pltpu.VMEM((3, tall, SIDE), f32),
            pltpu.VMEM((3 * rows + 2, PARTS, lanes), f32),
            pltpu.VMEM((BLOCKS, 3 * rows, PARTS, lanes), f32),
            pltpu.VMEM((6, 3 * rows, lanes), f32),
            pltpu.VMEM((6, 3 * rows, PARTS, lanes), f32),
            dma((6,)),
            dma((BLOCKS + 2,)),
        ],
        compiler_params=params,
        name="first",
    )(eps_table, fields, before, after, up, before_side, after_side)
    tiles = summed(sums)
    basis, solution, sums = pl.pallas_call(
        functools.partial(second_kernel, rows, cols),
        out_shape=[
            jax.ShapeDtypeStruct((BLOCKS, rows, PARTS, cols), f32),
            jax.ShapeDtypeStruct((rows, PARTS, cols), f32),
            jax.ShapeDtypeStruct((lat_size, PARTS, SIDE), f32),
        ],
        in_specs=[smem, vmem] + [anywhere] * 3,
        out_specs=[anywhere] * 2 + [vmem],
        scratch_shapes=[
            pltpu.VMEM((BLOCKS, 2 * rows, PARTS, lanes), f32),
            pltpu.VMEM((BLOCKS, 2 * rows, PARTS, lanes), f32),
            pltpu.VMEM((6, 2 * rows, PARTS, lanes), f32),
            pltpu.VMEM((rows, PARTS, cols), f32),
            pltpu.VMEM((2, ANGLES, BLOCKS, PARTS, SIDE), f32),
            dma((BLOCKS + 2,)),
            dma((BLOCKS + 1,)),
        ],
        compiler_params=params,
        name="second",
    )(eps_table, tiles, basis, spread, guess)
    tiles = summed(sums)
    solution, residual = pl.pallas_call(
        functools.partial(third_kernel, rows, cols),
        out_shape=[jax.ShapeDtypeStruct((count, cols), f32)] * 2,
        in_specs=[smem, vmem] + [anywhere] * 2,
        out_specs=[vmem] * 2,
        scratch_shapes=[
            pltpu.VMEM((2, rows, PARTS, cols), f32),
            pltpu.VMEM((BLOCKS, rows, PARTS, cols), f32),
            pltpu.VMEM((2, ANGLES, BLOCKS, PARTS, SIDE), f32),
            dma((BLOCKS + 1,)),
        ],
        compiler_params=params,
        name="third",
    )(eps_table, tiles, basis, solution)
    return solution.reshape(x_start.shape), residual.reshape(x_start.shape)


def solution(mesh):
    in_specs = (
        P(None, None, "lat", "dep"),
        P(None, None, "lat", "dep"),
        P(),
        P("lat", "dep"),
        P(None, "lat", "dep"),
    )
    out_specs = (P(None, None, "lat", "dep"), P(None, None, "lat", "dep"))
    return jax.shard_map(shards, mesh=mesh, in_specs=in_specs, out_specs=out_specs, check_vma=False)
```

```python
import functools

import jax
import jax.numpy as jnp
from jax import lax
from jax.experimental import pallas as pl
from jax.experimental.pallas import tpu as pltpu
from jax.sharding import PartitionSpec as P

S = 4
OUTER = 4
LABELS = 8
PML = 16
ANGLES = 4

sigma_peak = 4.0
k_squared = 2.0

FUSE = 2
POWERS = S * FUSE
BLOCKS = POWERS + 1
PARTS = 2 * ANGLES
HEIGHT = BLOCKS * PARTS
SCALE = 1.5
HIGH = lax.Precision.HIGHEST
SIDE = 128
EDGE = 18
TIERS = SIDE // EDGE
GROUP = 24
MIB = 1024 * 1024


def shifts_of(table):
    real, imag = [sum(table[part, k] for k in range(LABELS)) * (1.0 / LABELS) for part in range(2)]
    root = 0.25 * imag + 0.12
    return 1.25 - 0.25 * real, root * root


def dot(a, b, dims):
    return lax.dot_general(a, b, (dims, ((), ())), precision=HIGH, preferred_element_type=jnp.float32)


def iota(shape, dim):
    return lax.broadcasted_iota(jnp.int32, shape, dim)


def coefficients(labels, level_lat, level_dep, table, shift):
    eps_real = jnp.zeros_like(labels)
    eps_imag = jnp.zeros_like(labels)
    for k in range(LABELS):
        here = labels == float(k + 1)
        eps_real = jnp.where(here, table[0, k], eps_real)
        eps_imag = jnp.where(here, table[1, k], eps_imag)

    def stretch_of(level):
        sigma = sigma_peak * (level * (1.0 / PML)) ** 2
        inverse = 1.0 / (1.0 + sigma * sigma)
        return inverse, -sigma * inverse

    lat_real, lat_imag = stretch_of(level_lat)
    dep_real, dep_imag = stretch_of(level_dep)
    centre_real = (lat_real + dep_real) * 0.25 - k_squared / 8.0 * eps_real + (1.0 - shift)
    centre_imag = (lat_imag + dep_imag) * 0.25 - k_squared / 8.0 * eps_imag
    side = -0.125 * SCALE
    found = (
        SCALE * centre_real,
        side * lat_real,
        side * dep_real,
        SCALE * centre_imag,
        side * lat_imag,
        side * dep_imag,
    )
    return [jnp.where(labels > 0.5, f, 0.0) for f in found]


def by_cells(fields, rows):
    return jnp.swapaxes(fields.reshape(PARTS, rows, fields.shape[1]), 0, 1)


def by_fields(cells):
    return jnp.swapaxes(cells, 0, 1).reshape(-1, cells.shape[2])


def spread_rows(compact, spread, first, count):
    sign = jnp.where(iota((PARTS, 1), 0) < ANGLES, 1.0, -1.0)

    for x in range(first, first + count):
        for k in range(6):
            line = jnp.broadcast_to(compact[k, x : x + 1, :], spread.shape[2:])
            spread[k, x] = line * sign if k >= 3 else line


def scaled_operator(middle, before, after, factors):
    lanes = middle.shape[1]
    lat = before + after
    dep = pltpu.roll(middle, 1, 1) + pltpu.roll(middle, lanes - 1, 1)
    straight = factors[0] * middle + factors[1] * lat + factors[2] * dep
    crossed = factors[3] * middle + factors[4] * lat + factors[5] * dep
    return straight + pltpu.roll(crossed, ANGLES, 0)


def by_groups(first, last, some):
    full = (last - first) // GROUP
    lax.fori_loop(0, full, lambda t, _: some(first + t * GROUP, GROUP), None)
    if (last - first) % GROUP:
        some(first + full * GROUP, (last - first) % GROUP)


def next_block(basis, spread, j, pair):
    rows = basis.shape[1]

    def some(base, count):
        made = []
        for i in range(count):
            x = base + i
            new = scaled_operator(
                basis[j, x], basis[j, x - 1], basis[j, x + 1], [spread[k, x] for k in range(6)]
            )
            if j % 2 == 1:
                new = new + pair * basis[j - 1, x]
            made.append(new)
        for i in range(count):
            basis[j + 1, base + i] = made[i]

    by_groups(j + 1, rows - 1 - j, some)


def packed_gram(basis, first, rows, cols):
    full = jnp.zeros((HEIGHT, HEIGHT), jnp.float32)
    for x in range(rows):
        block = basis[:, first + x, :, 0:cols].reshape(HEIGHT, cols)
        full = full + dot(block, block, ((1,), (1,)))
    full = jnp.concatenate([full, jnp.zeros((HEIGHT, SIDE - HEIGHT), jnp.float32)], axis=1)
    both = full + pltpu.roll(pltpu.roll(full, SIDE - ANGLES, 1), HEIGHT - ANGLES, 0)
    tile = jnp.zeros((PARTS, SIDE), jnp.float32)
    for j in range(BLOCKS):
        low, move = PLACES[j]
        upper = jnp.where(upper_lanes(j), both[PARTS * j : PARTS * (j + 1)], 0.0)
        upper = pltpu.roll(upper, move % SIDE, 1) if move else upper
        tile = tile + (pltpu.roll(upper, ANGLES, 0) if low else upper)
    return tile


PLACES = {
    0: (False, 0),
    3: (False, 72 - 24),
    8: (False, 120 - 64),
    1: (False, 0 - 8 + ANGLES),
    2: (False, 64 - 16 + ANGLES),
    4: (True, 0 - 32),
    5: (True, 40 - 40),
    6: (True, 72 - 48),
    7: (True, 96 - 56),
}


def upper_lanes(j):
    row, lane = iota((PARTS, SIDE), 0), iota((PARTS, SIDE), 1)
    return (row < ANGLES) & (lane % PARTS < ANGLES) & (lane >= PARTS * j) & (lane < HEIGHT)


def half_gram(tile):
    lane = iota((PARTS, SIDE), 1)
    parts = []
    for j in range(BLOCKS):
        low, move = PLACES[j]
        back = pltpu.roll(tile, ANGLES, 0) if low else tile
        back = pltpu.roll(back, -move % SIDE, 1) if move else back
        weight = jnp.where(lane < PARTS * (j + 1), 0.5, 1.0)
        parts.append(jnp.where(upper_lanes(j), back * weight, 0.0))
    return jnp.concatenate(parts, axis=0)


def solve_normal(gram):
    size = S * ANGLES
    work = gram[0:24]
    work = pltpu.roll(work, 24 - ANGLES, 0)[0:size]
    row, lane = iota((size, SIDE), 0), iota((size, SIDE), 1)
    diagonal = jnp.where(lane == row + ANGLES, work, 0.0)
    by_row = lax.rsqrt(jnp.sum(diagonal, axis=1, keepdims=True))
    by_lane = jnp.sum(diagonal, axis=0, keepdims=True)
    by_lane = jnp.where(
        (lane[0:1] >= ANGLES) & (lane[0:1] < ANGLES + size), lax.rsqrt(jnp.where(by_lane > 0.0, by_lane, 1.0)), 1.0
    )
    work = work * by_row * by_lane
    left = [jnp.broadcast_to(work[:, i : i + 1], (size, SIDE)) for i in range(ANGLES, ANGLES + size)] + [work]
    for k in range(0, size, 2):
        one, two = left[0], left[1]
        a, b, c, d = one[k : k + 1], two[k : k + 1], one[k + 1 : k + 2], two[k + 1 : k + 2]
        inverse = 1.0 / (a * d - b * c)
        a, b, c, d = a * inverse, b * inverse, c * inverse, d * inverse
        one, two = one - jnp.where(row == k, 1.0, 0.0), two - jnp.where(row == k + 1, 1.0, 0.0)
        after = []
        for column in left[2:]:
            upper, lower = column[k : k + 1], column[k + 1 : k + 2]
            after.append(column - one * (d * upper - b * lower) - two * (a * lower - c * upper))
        left = after
    return jnp.where(lane < ANGLES, left[0] * by_row, 0.0)


def cycles(tile, shift, pair):
    upper = half_gram(tile)
    row, lane = iota((HEIGHT, SIDE), 0), iota((HEIGHT, SIDE), 1)
    even = jnp.where(((row // PARTS) % 2 == 0) & (row < HEIGHT - PARTS), pair * SCALE, 0.0)
    residual = jnp.where((row == lane) & (lane < ANGLES), 1.0, 0.0)
    update = jnp.zeros((HEIGHT, SIDE), jnp.float32)
    blank = jnp.zeros((SIDE - HEIGHT, SIDE), jnp.float32)
    for cycle in range(FUSE):
        power = residual
        powers = residual
        for k in range(1, S + 1):
            power = (
                pltpu.roll(power, PARTS, 0) * (1.0 / SCALE)
                + power * shift
                - pltpu.roll(power, HEIGHT - PARTS, 0) * even
            )
            powers = powers + pltpu.roll(power, ANGLES * k, 1)
        half = dot(upper, jnp.concatenate([powers, blank], axis=0), ((1,), (0,)))
        gram = dot(powers, half, ((0,), (0,))) + dot(half, powers, ((0,), (0,)))
        mixing = solve_normal(gram)
        size = S * ANGLES
        low = jnp.concatenate([mixing, jnp.zeros((24 - size, SIDE), jnp.float32)], axis=0)
        high = pltpu.roll(pltpu.roll(low, ANGLES, 0), ANGLES, 1)
        both = jnp.concatenate([low + high, jnp.zeros((SIDE - 24, SIDE), jnp.float32)], axis=0)
        change = dot(powers, both, ((1,), (0,)))
        update = update + jnp.where(lane < ANGLES, change, 0.0)
        residual = residual - jnp.where(lane < ANGLES, pltpu.roll(change, SIDE - ANGLES, 1), 0.0)
    return update, residual


def set_weights(weights, which, table):
    row, lane = iota((HEIGHT, SIDE), 0), iota((HEIGHT, SIDE), 1)
    for d in range(ANGLES):
        picked = jnp.where(lane == (row - d + ANGLES) % ANGLES, table, 0.0)
        picked = jnp.broadcast_to(jnp.sum(picked, axis=1, keepdims=True), (HEIGHT, SIDE))
        for j in range(BLOCKS):
            single = picked[PARTS * j : PARTS * (j + 1)]
            weights[which, d, j] = single + pltpu.roll(single, ANGLES, 0)


def mixed(weights, which, blocks):
    lanes = blocks[0].shape[1]
    angle = iota((PARTS, lanes), 0) % ANGLES
    total = None
    for d in range(ANGLES):
        turned = None
        for j, block in enumerate(blocks):
            factor = weights[which, d, j]
            term = jnp.concatenate([factor] * (lanes // SIDE), axis=1) * block
            turned = term if turned is None else turned + term
        if d:
            turned = jnp.where(
                angle + d < ANGLES, pltpu.roll(turned, PARTS - d, 0), pltpu.roll(turned, ANGLES - d, 0)
            )
        total = turned if total is None else total + turned
    return total


def fetch(source, target, sem):
    copy = pltpu.make_async_copy(source, target, sem)
    copy.start()
    return copy


def packed_rows(height):
    return -(-height // (TIERS * 8)) * 8


def pack_kernel(rows, cols, start, source, labels, levels, fields, first, last):
    size = PARTS * rows
    height = fields.shape[0]
    fields[0:size, :] = start[...]
    fields[size : 2 * size, :] = source[...]
    fields[2 * size : 2 * size + rows, :] = (labels[...] + 1).astype(jnp.float32)
    fields[2 * size + rows : height, :] = levels[...].astype(jnp.float32)
    tall = packed_rows(height)
    lane = iota((tall, SIDE), 1)
    for out, at, keep, origin in ((first, 0, lane < EDGE, 0), (last, cols - SIDE, lane >= SIDE - EDGE, SIDE - EDGE)):
        total = jnp.zeros((tall, SIDE), jnp.float32)
        for g in range(TIERS):
            top = g * tall
            part = fields[top : min(top + tall, height), at : at + SIDE]
            if part.shape[0] < tall:
                part = jnp.concatenate([part, jnp.zeros((tall - part.shape[0], SIDE), jnp.float32)], axis=0)
            total = total + pltpu.roll(jnp.where(keep, part, 0.0), (EDGE * g - origin) % SIDE, 1)
        out[...] = total


def unpack_side(packed, out):
    height = out.shape[0]
    tall = packed_rows(height)
    lane = iota((tall, SIDE), 1)
    right, left = packed[0:tall, :], packed[tall : 2 * tall, :]
    for g in range(TIERS):
        part = jnp.where(lane < EDGE, pltpu.roll(right, -EDGE * g % SIDE, 1), 0.0)
        part = part + jnp.where(lane >= SIDE - EDGE, pltpu.roll(left, (SIDE - EDGE - EDGE * g) % SIDE, 1), 0.0)
        top = g * tall
        count = min(tall, height - top)
        out[top : top + count, :] = part[0:count]


def side_kernel(rows, cols, right, left, before, after, up, down, ends, sems):
    size = right.shape[0]
    copies = []
    for f in range(PARTS):
        copies.append(fetch(before.at[pl.ds((f + 1) * rows - 8, 8)], ends.at[0, f], sems.at[f]))
        copies.append(fetch(after.at[pl.ds(f * rows, 8)], ends.at[1, f], sems.at[PARTS + f]))
    for out in (up, down):
        out[0:size, :] = right[...]
        out[size : 2 * size, :] = left[...]
    for copy in copies:
        copy.wait()
    for out, p, row in ((up, 0, 7), (down, 1, 0)):
        far = jnp.concatenate([ends[p, f, row : row + 1, :] for f in range(PARTS)], axis=0)
        for t in range(cols // SIDE):
            out[2 * size + t * PARTS : 2 * size + (t + 1) * PARTS, :] = far[:, t * SIDE : (t + 1) * SIDE]


def first_kernel(
    rows, cols, table, own, before, after, own_side, before_side, after_side, basis_out, compact_out, guess_out, sums,
    mains, packed, sides, guess, basis, compact, spread, in_sems, out_sems,
):
    lanes = cols + SIDE
    shift, pair = shifts_of(table)
    fields = PARTS * rows
    parts = ((1, own, own_side), (0, before, before_side), (2, after, after_side))
    copies = {}
    for p, main, side in parts:
        copies[p] = [fetch(main, mains.at[p], in_sems.at[p]), fetch(side, packed.at[p], in_sems.at[3 + p])]
    for p, _, _ in parts:
        for copy in copies[p]:
            copy.wait()
        unpack_side(packed.at[p], sides.at[p])
        for at, ref in ((0, mains.at[p]), (cols, sides.at[p])):
            size = ref.shape[1]
            guess[pl.ds(1 + p * rows, rows), :, at : at + size] = by_cells(ref[0:fields, :], rows)
            basis[0, pl.ds(p * rows, rows), :, at : at + size] = by_cells(ref[fields : 2 * fields, :], rows)
            level = [ref[2 * fields + k * rows : 2 * fields + (k + 1) * rows, :] for k in range(3)]
            found = coefficients(*level, table, shift)
            for k in range(6):
                compact[k, p * rows : (p + 1) * rows, at : at + size] = found[k]
        spread_rows(compact, spread, p * rows, rows)
    end = packed.shape[1] - cols // SIDE * PARTS
    for x, p in ((0, 0), (3 * rows + 1, 2)):
        for t in range(cols // SIDE):
            guess[x, :, t * SIDE : (t + 1) * SIDE] = packed[p, end + t * PARTS : end + (t + 1) * PARTS, :]
        guess[x, :, cols:lanes] = jnp.zeros((PARTS, SIDE), jnp.float32)
    half = rows // 2
    outs = [fetch(guess.at[pl.ds(rows + 1, rows), :, pl.ds(0, cols)], guess_out, out_sems.at[BLOCKS])]
    outs.append(fetch(compact.at[:, pl.ds(half, 2 * rows)], compact_out, out_sems.at[BLOCKS + 1]))

    def start(base, count):
        made = []
        for i in range(count):
            x = base + i
            middle = guess[x + 1]
            applied = scaled_operator(middle, guess[x], guess[x + 2], [spread[k, x] for k in range(6)])
            made.append(basis[0, x] - applied * (1.0 / SCALE) - shift * middle)
        for i in range(count):
            basis[0, base + i] = made[i]

    by_groups(0, 3 * rows, start)
    outs.append(fetch(basis.at[0, pl.ds(half, 2 * rows)], basis_out.at[0], out_sems.at[0]))
    for j in range(POWERS):
        next_block(basis, spread, j, pair * SCALE * SCALE)
        outs.append(fetch(basis.at[j + 1, pl.ds(half, 2 * rows)], basis_out.at[j + 1], out_sems.at[j + 1]))
    tile = packed_gram(basis, rows, rows, cols)
    for i in range(sums.shape[0]):
        sums[i] = tile
    for copy in outs:
        copy.wait()


def second_kernel(
    rows, cols, table, tiles, basis_in, compact_in, guess_in, basis_out, solution_out, sums, old, basis, compact, spread,
    guess, weights, in_sems, out_sems,
):
    shift, pair = shifts_of(table)
    factors = fetch(compact_in, compact, in_sems.at[BLOCKS + 1])
    copies = [fetch(basis_in.at[j], old.at[j], in_sems.at[j]) for j in range(BLOCKS)]
    copies.append(fetch(guess_in, guess, in_sems.at[BLOCKS]))
    half = rows // 2
    factors.wait()
    spread_rows(compact, spread, 0, 2 * rows)
    update, residual = cycles(jnp.sum(tiles[...], axis=0), shift, pair)
    set_weights(weights, 0, residual)
    set_weights(weights, 1, update)
    for copy in copies:
        copy.wait()

    def one(t, _):
        for i in range(4):
            x = 4 * t + i
            basis[0, x] = mixed(weights, 0, [old[j, x] for j in range(BLOCKS)])

    lax.fori_loop(0, 2 * rows // 4, one, None)

    def move(t, _):
        for i in range(4):
            x = 4 * t + i
            guess[x] = guess[x] + mixed(weights, 1, [old[j, half + x, :, 0:cols] for j in range(POWERS)])

    lax.fori_loop(0, rows // 4, move, None)
    outs = [fetch(guess, solution_out, out_sems.at[BLOCKS])]
    inside = (pl.ds(half, rows), slice(None), pl.ds(0, cols))
    outs.append(fetch(basis.at[(0, *inside)], basis_out.at[0], out_sems.at[0]))
    for j in range(POWERS):
        next_block(basis, spread, j, pair * SCALE * SCALE)
        outs.append(fetch(basis.at[(j + 1, *inside)], basis_out.at[j + 1], out_sems.at[j + 1]))
    tile = packed_gram(basis, half, rows, cols)
    for i in range(sums.shape[0]):
        sums[i] = tile
    for copy in outs:
        copy.wait()


def third_kernel(rows, cols, table, tiles, basis_in, start_in, solution, residual, made, old, weights, in_sems):
    shift, pair = shifts_of(table)
    copies = [fetch(basis_in.at[j], old.at[j], in_sems.at[j]) for j in range(BLOCKS)]
    copies.append(fetch(start_in, made.at[1], in_sems.at[BLOCKS]))
    update, left = cycles(jnp.sum(tiles[...], axis=0), shift, pair)
    set_weights(weights, 0, left)
    set_weights(weights, 1, update)
    for copy in copies:
        copy.wait()

    def move(t, _):
        for i in range(4):
            x = 4 * t + i
            blocks = [old[j, x] for j in range(BLOCKS)]
            made[0, x] = mixed(weights, 0, blocks)
            made[1, x] = made[1, x] + mixed(weights, 1, blocks[:POWERS])

    lax.fori_loop(0, rows // 4, move, None)
    residual[...] = by_fields(made[0])
    solution[...] = by_fields(made[1])


def summed(copies):
    got = lax.all_to_all(copies, "lat", 0, 0, tiled=True)
    near = jnp.sum(got, axis=0)
    sent = jnp.broadcast_to(near[None], (lax.axis_size("dep"),) + near.shape)
    return lax.all_to_all(sent, "dep", 0, 0, tiled=True)


def shards(x_start, source, eps_table, labels, pml_level):
    rows, cols = labels.shape
    lanes = cols + SIDE
    f32 = jnp.float32
    vmem = pl.BlockSpec(memory_space=pltpu.VMEM)
    smem = pl.BlockSpec(memory_space=pltpu.SMEM)
    anywhere = pl.BlockSpec(memory_space=pl.ANY)

    def params(mib):
        return pltpu.CompilerParams(vmem_limit_bytes=mib * MIB)

    lat_size = lax.axis_size("lat")
    start = x_start.reshape(PARTS * rows, cols)
    height = (2 * PARTS + 3) * rows
    count = PARTS * rows
    dma = pltpu.SemaphoreType.DMA
    tall = packed_rows(height)
    fields, first, last = pl.pallas_call(
        functools.partial(pack_kernel, rows, cols),
        out_shape=[
            jax.ShapeDtypeStruct((height, cols), f32),
            jax.ShapeDtypeStruct((tall, SIDE), f32),
            jax.ShapeDtypeStruct((tall, SIDE), f32),
        ],
        in_specs=[vmem] * 4,
        out_specs=[vmem] * 3,
        compiler_params=params(8),
        name="pack",
    )(start, source.reshape(count, cols), labels, pml_level.reshape(2 * rows, cols))

    def along(array, axis, step):
        size = lax.axis_size(axis)
        return lax.ppermute(array, axis, [(i, i + step) for i in range(size) if 0 <= i + step < size])

    before, after = along(fields, "lat", 1), along(fields, "lat", -1)
    right, left = along(first, "dep", -1), along(last, "dep", 1)
    both = 2 * tall + cols // SIDE * PARTS
    up, down = pl.pallas_call(
        functools.partial(side_kernel, rows, cols),
        out_shape=[jax.ShapeDtypeStruct((both, SIDE), f32)] * 2,
        in_specs=[vmem, vmem, anywhere, anywhere],
        out_specs=[vmem] * 2,
        scratch_shapes=[pltpu.VMEM((2, PARTS, 8, cols), f32), dma((2 * PARTS,))],
        compiler_params=params(4),
        name="side",
    )(right, left, before, after)
    before_side, after_side = along(up, "lat", 1), along(down, "lat", -1)

    basis, compact, guess, sums = pl.pallas_call(
        functools.partial(first_kernel, rows, cols),
        out_shape=[
            jax.ShapeDtypeStruct((BLOCKS, 2 * rows, PARTS, lanes), f32),
            jax.ShapeDtypeStruct((6, 2 * rows, lanes), f32),
            jax.ShapeDtypeStruct((rows, PARTS, cols), f32),
            jax.ShapeDtypeStruct((lat_size, PARTS, SIDE), f32),
        ],
        in_specs=[smem] + [anywhere] * 6,
        out_specs=[anywhere] * 3 + [vmem],
        scratch_shapes=[
            pltpu.VMEM((3, height, cols), f32),
            pltpu.VMEM((3, both, SIDE), f32),
            pltpu.VMEM((3, height, SIDE), f32),
            pltpu.VMEM((3 * rows + 2, PARTS, lanes), f32),
            pltpu.VMEM((BLOCKS, 3 * rows, PARTS, lanes), f32),
            pltpu.VMEM((6, 3 * rows, lanes), f32),
            pltpu.VMEM((6, 3 * rows, PARTS, lanes), f32),
            dma((6,)),
            dma((BLOCKS + 2,)),
        ],
        compiler_params=params(26),
        name="first",
    )(eps_table, fields, before, after, up, before_side, after_side)
    tiles = summed(sums)
    basis, solution, sums = pl.pallas_call(
        functools.partial(second_kernel, rows, cols),
        out_shape=[
            jax.ShapeDtypeStruct((BLOCKS, rows, PARTS, cols), f32),
            jax.ShapeDtypeStruct((rows, PARTS, cols), f32),
            jax.ShapeDtypeStruct((lat_size, PARTS, SIDE), f32),
        ],
        in_specs=[smem, vmem] + [anywhere] * 3,
        out_specs=[anywhere] * 2 + [vmem],
        scratch_shapes=[
            pltpu.VMEM((BLOCKS, 2 * rows, PARTS, lanes), f32),
            pltpu.VMEM((BLOCKS, 2 * rows, PARTS, lanes), f32),
            pltpu.VMEM((6, 2 * rows, lanes), f32),
            pltpu.VMEM((6, 2 * rows, PARTS, lanes), f32),
            pltpu.VMEM((rows, PARTS, cols), f32),
            pltpu.VMEM((2, ANGLES, BLOCKS, PARTS, SIDE), f32),
            dma((BLOCKS + 2,)),
            dma((BLOCKS + 1,)),
        ],
        compiler_params=params(24),
        name="second",
    )(eps_table, tiles, basis, compact, guess)
    tiles = summed(sums)
    solution, residual = pl.pallas_call(
        functools.partial(third_kernel, rows, cols),
        out_shape=[jax.ShapeDtypeStruct((count, cols), f32)] * 2,
        in_specs=[smem, vmem] + [anywhere] * 2,
        out_specs=[vmem] * 2,
        scratch_shapes=[
            pltpu.VMEM((2, rows, PARTS, cols), f32),
            pltpu.VMEM((BLOCKS, rows, PARTS, cols), f32),
            pltpu.VMEM((2, ANGLES, BLOCKS, PARTS, SIDE), f32),
            dma((BLOCKS + 1,)),
        ],
        compiler_params=params(8),
        name="third",
    )(eps_table, tiles, basis, solution)
    return solution.reshape(x_start.shape), residual.reshape(x_start.shape)


def solution(mesh):
    in_specs = (
        P(None, None, "lat", "dep"),
        P(None, None, "lat", "dep"),
        P(),
        P("lat", "dep"),
        P(None, "lat", "dep"),
    )
    out_specs = (P(None, None, "lat", "dep"), P(None, None, "lat", "dep"))
    return jax.shard_map(shards, mesh=mesh, in_specs=in_specs, out_specs=out_specs, check_vma=False)
```

```python
import functools

import jax
import jax.numpy as jnp
from jax import lax
from jax.experimental import pallas as pl
from jax.experimental.pallas import tpu as pltpu
from jax.sharding import PartitionSpec as P

S = 4
OUTER = 4
LABELS = 8
PML = 16
ANGLES = 4

sigma_peak = 4.0
k_squared = 2.0

FUSE = 2
POWERS = S * FUSE
BLOCKS = POWERS + 1
PARTS = 2 * ANGLES
HEIGHT = BLOCKS * PARTS
SCALE = 1.5
HIGH = lax.Precision.HIGHEST
SIDE = 128
EDGE = 18
TIERS = SIDE // EDGE
GROUP = 24
MIB = 1024 * 1024


def shifts_of(table):
    real, imag = [sum(table[part, k] for k in range(LABELS)) * (1.0 / LABELS) for part in range(2)]
    root = 0.25 * imag + 0.12
    return 1.25 - 0.25 * real, root * root


def dot(a, b, dims):
    return lax.dot_general(a, b, (dims, ((), ())), precision=HIGH, preferred_element_type=jnp.float32)


def iota(shape, dim):
    return lax.broadcasted_iota(jnp.int32, shape, dim)


def spread_scalar(scalars, i, shape):
    return jnp.concatenate([jnp.broadcast_to(scalars[i : i + 1, :], (shape[0], SIDE))] * (shape[1] // SIDE), axis=1)


SHIFT, PAIR = 2 * LABELS, 2 * LABELS + 1


def coefficients(labels, level_lat, level_dep, scalars):
    eps_real = jnp.zeros_like(labels)
    eps_imag = jnp.zeros_like(labels)
    for k in range(LABELS):
        here = labels == float(k + 1)
        eps_real = jnp.where(here, spread_scalar(scalars, k, labels.shape), eps_real)
        eps_imag = jnp.where(here, spread_scalar(scalars, LABELS + k, labels.shape), eps_imag)

    def stretch_of(level):
        sigma = sigma_peak * (level * (1.0 / PML)) ** 2
        inverse = 1.0 / (1.0 + sigma * sigma)
        return inverse, -sigma * inverse

    lat_real, lat_imag = stretch_of(level_lat)
    dep_real, dep_imag = stretch_of(level_dep)
    centre_real = (lat_real + dep_real) * 0.25 - k_squared / 8.0 * eps_real
    centre_real = centre_real + (1.0 - spread_scalar(scalars, SHIFT, labels.shape))
    centre_imag = (lat_imag + dep_imag) * 0.25 - k_squared / 8.0 * eps_imag
    side = -0.125 * SCALE
    found = (
        SCALE * centre_real,
        side * lat_real,
        side * dep_real,
        SCALE * centre_imag,
        side * lat_imag,
        side * dep_imag,
    )
    return [jnp.where(labels > 0.5, f, 0.0) for f in found]


def by_cells(fields, rows):
    return jnp.swapaxes(fields.reshape(PARTS, rows, fields.shape[1]), 0, 1)


def by_fields(cells):
    return jnp.swapaxes(cells, 0, 1).reshape(-1, cells.shape[2])


def spread_rows(compact, spread, first, count):
    sign = jnp.where(iota((PARTS, 1), 0) < ANGLES, 1.0, -1.0)

    for x in range(first, first + count):
        for k in range(6):
            line = jnp.broadcast_to(compact[k, x : x + 1, :], spread.shape[2:])
            spread[k, x] = line * sign if k >= 3 else line


def scaled_operator(middle, before, after, factors):
    lanes = middle.shape[1]
    lat = before + after
    dep = pltpu.roll(middle, 1, 1) + pltpu.roll(middle, lanes - 1, 1)
    straight = factors[0] * middle + factors[1] * lat + factors[2] * dep
    crossed = factors[3] * middle + factors[4] * lat + factors[5] * dep
    return straight + pltpu.roll(crossed, ANGLES, 0)


def by_groups(first, last, some):
    full = (last - first) // GROUP
    lax.fori_loop(0, full, lambda t, _: some(first + t * GROUP, GROUP), None)
    if (last - first) % GROUP:
        some(first + full * GROUP, (last - first) % GROUP)


def next_block(basis, spread, j, pair):
    rows = basis.shape[1]

    def some(base, count):
        made = []
        for i in range(count):
            x = base + i
            new = scaled_operator(
                basis[j, x], basis[j, x - 1], basis[j, x + 1], [spread[k, x] for k in range(6)]
            )
            if j % 2 == 1:
                new = new + pair * basis[j - 1, x]
            made.append(new)
        for i in range(count):
            basis[j + 1, base + i] = made[i]

    by_groups(j + 1, rows - 1 - j, some)


def packed_gram(basis, first, rows, cols):
    full = jnp.zeros((HEIGHT, HEIGHT), jnp.float32)
    for x in range(rows):
        block = basis[:, first + x, :, 0:cols].reshape(HEIGHT, cols)
        full = full + dot(block, block, ((1,), (1,)))
    full = jnp.concatenate([full, jnp.zeros((HEIGHT, SIDE - HEIGHT), jnp.float32)], axis=1)
    both = full + pltpu.roll(pltpu.roll(full, SIDE - ANGLES, 1), HEIGHT - ANGLES, 0)
    tile = jnp.zeros((PARTS, SIDE), jnp.float32)
    for j in range(BLOCKS):
        low, move = PLACES[j]
        upper = jnp.where(upper_lanes(j), both[PARTS * j : PARTS * (j + 1)], 0.0)
        upper = pltpu.roll(upper, move % SIDE, 1) if move else upper
        tile = tile + (pltpu.roll(upper, ANGLES, 0) if low else upper)
    return tile


PLACES = {
    0: (False, 0),
    3: (False, 72 - 24),
    8: (False, 120 - 64),
    1: (False, 0 - 8 + ANGLES),
    2: (False, 64 - 16 + ANGLES),
    4: (True, 0 - 32),
    5: (True, 40 - 40),
    6: (True, 72 - 48),
    7: (True, 96 - 56),
}


def upper_lanes(j):
    row, lane = iota((PARTS, SIDE), 0), iota((PARTS, SIDE), 1)
    return (row < ANGLES) & (lane % PARTS < ANGLES) & (lane >= PARTS * j) & (lane < HEIGHT)


def half_gram(tile):
    lane = iota((PARTS, SIDE), 1)
    parts = []
    for j in range(BLOCKS):
        low, move = PLACES[j]
        back = pltpu.roll(tile, ANGLES, 0) if low else tile
        back = pltpu.roll(back, -move % SIDE, 1) if move else back
        weight = jnp.where(lane < PARTS * (j + 1), 0.5, 1.0)
        parts.append(jnp.where(upper_lanes(j), back * weight, 0.0))
    return jnp.concatenate(parts, axis=0)


def solve_normal(gram):
    size = S * ANGLES
    work = gram[0:24]
    work = pltpu.roll(work, 24 - ANGLES, 0)[0:size]
    row, lane = iota((size, SIDE), 0), iota((size, SIDE), 1)
    diagonal = jnp.where(lane == row + ANGLES, work, 0.0)
    by_row = lax.rsqrt(jnp.sum(diagonal, axis=1, keepdims=True))
    by_lane = jnp.sum(diagonal, axis=0, keepdims=True)
    by_lane = jnp.where(
        (lane[0:1] >= ANGLES) & (lane[0:1] < ANGLES + size), lax.rsqrt(jnp.where(by_lane > 0.0, by_lane, 1.0)), 1.0
    )
    work = work * by_row * by_lane
    left = [jnp.broadcast_to(work[:, i : i + 1], (size, SIDE)) for i in range(ANGLES, ANGLES + size)] + [work]
    for k in range(0, size, 2):
        one, two = left[0], left[1]
        a, b, c, d = one[k : k + 1], two[k : k + 1], one[k + 1 : k + 2], two[k + 1 : k + 2]
        inverse = 1.0 / (a * d - b * c)
        a, b, c, d = a * inverse, b * inverse, c * inverse, d * inverse
        one, two = one - jnp.where(row == k, 1.0, 0.0), two - jnp.where(row == k + 1, 1.0, 0.0)
        after = []
        for column in left[2:]:
            upper, lower = column[k : k + 1], column[k + 1 : k + 2]
            after.append(column - one * (d * upper - b * lower) - two * (a * lower - c * upper))
        left = after
    return jnp.where(lane < ANGLES, left[0] * by_row, 0.0)


def cycles(tile, shift, pair):
    upper = half_gram(tile)
    row, lane = iota((HEIGHT, SIDE), 0), iota((HEIGHT, SIDE), 1)
    even = jnp.where(((row // PARTS) % 2 == 0) & (row < HEIGHT - PARTS), pair * SCALE, 0.0)
    residual = jnp.where((row == lane) & (lane < ANGLES), 1.0, 0.0)
    update = jnp.zeros((HEIGHT, SIDE), jnp.float32)
    blank = jnp.zeros((SIDE - HEIGHT, SIDE), jnp.float32)
    for cycle in range(FUSE):
        power = residual
        powers = residual
        for k in range(1, S + 1):
            power = (
                pltpu.roll(power, PARTS, 0) * (1.0 / SCALE)
                + power * shift
                - pltpu.roll(power, HEIGHT - PARTS, 0) * even
            )
            powers = powers + pltpu.roll(power, ANGLES * k, 1)
        half = dot(upper, jnp.concatenate([powers, blank], axis=0), ((1,), (0,)))
        gram = dot(powers, half, ((0,), (0,))) + dot(half, powers, ((0,), (0,)))
        mixing = solve_normal(gram)
        size = S * ANGLES
        low = jnp.concatenate([mixing, jnp.zeros((24 - size, SIDE), jnp.float32)], axis=0)
        high = pltpu.roll(pltpu.roll(low, ANGLES, 0), ANGLES, 1)
        both = jnp.concatenate([low + high, jnp.zeros((SIDE - 24, SIDE), jnp.float32)], axis=0)
        change = dot(powers, both, ((1,), (0,)))
        update = update + jnp.where(lane < ANGLES, change, 0.0)
        residual = residual - jnp.where(lane < ANGLES, pltpu.roll(change, SIDE - ANGLES, 1), 0.0)
    return update, residual


def set_weights(weights, which, table):
    row, lane = iota((HEIGHT, SIDE), 0), iota((HEIGHT, SIDE), 1)
    for d in range(ANGLES):
        picked = jnp.where(lane == (row - d + ANGLES) % ANGLES, table, 0.0)
        picked = jnp.broadcast_to(jnp.sum(picked, axis=1, keepdims=True), (HEIGHT, SIDE))
        for j in range(BLOCKS):
            single = picked[PARTS * j : PARTS * (j + 1)]
            weights[which, d, j] = single + pltpu.roll(single, ANGLES, 0)


def mixed(weights, which, blocks):
    lanes = blocks[0].shape[1]
    angle = iota((PARTS, lanes), 0) % ANGLES
    total = None
    for d in range(ANGLES):
        turned = None
        for j, block in enumerate(blocks):
            factor = weights[which, d, j]
            term = jnp.concatenate([factor] * (lanes // SIDE), axis=1) * block
            turned = term if turned is None else turned + term
        if d:
            turned = jnp.where(
                angle + d < ANGLES, pltpu.roll(turned, PARTS - d, 0), pltpu.roll(turned, ANGLES - d, 0)
            )
        total = turned if total is None else total + turned
    return total


def fetch(source, target, sem):
    copy = pltpu.make_async_copy(source, target, sem)
    copy.start()
    return copy


def packed_rows(height):
    return -(-height // (TIERS * 8)) * 8


def pack_kernel(rows, cols, table_in, start, source, labels, levels, fields, first, last, scalars, table, marks, sems):
    size = PARTS * rows
    height = fields.shape[0]
    copies = [
        fetch(labels, marks.at[pl.ds(0, rows)], sems.at[0]),
        fetch(levels, marks.at[pl.ds(rows, 2 * rows)], sems.at[1]),
        fetch(start, fields.at[pl.ds(0, size)], sems.at[2]),
        fetch(source, fields.at[pl.ds(size, size)], sems.at[3]),
        fetch(table_in, table, sems.at[4]),
    ]
    for copy in copies:
        copy.wait()
    fields[2 * size : 2 * size + rows, :] = (marks[0:rows, :] + 1).astype(jnp.float32)
    fields[2 * size + rows : height, :] = marks[rows:, :].astype(jnp.float32)
    row = iota(scalars.shape, 0)
    known = jnp.zeros(scalars.shape, jnp.float32)
    for i, value in enumerate([table[p, k] for p in range(2) for k in range(LABELS)] + list(shifts_of(table))):
        known = jnp.where(row == i, value, known)
    scalars[...] = known
    tall = packed_rows(height)
    lane = iota((tall, SIDE), 1)
    for out, at, keep, origin in ((first, 0, lane < EDGE, 0), (last, cols - SIDE, lane >= SIDE - EDGE, SIDE - EDGE)):
        total = jnp.zeros((tall, SIDE), jnp.float32)
        for g in range(TIERS):
            top = g * tall
            part = fields[top : min(top + tall, height), at : at + SIDE]
            if part.shape[0] < tall:
                part = jnp.concatenate([part, jnp.zeros((tall - part.shape[0], SIDE), jnp.float32)], axis=0)
            total = total + pltpu.roll(jnp.where(keep, part, 0.0), (EDGE * g - origin) % SIDE, 1)
        out[...] = total


def unpack_side(packed, out):
    height = out.shape[0]
    tall = packed_rows(height)
    lane = iota((tall, SIDE), 1)
    right, left = packed[0:tall, :], packed[tall : 2 * tall, :]
    for g in range(TIERS):
        part = jnp.where(lane < EDGE, pltpu.roll(right, -EDGE * g % SIDE, 1), 0.0)
        part = part + jnp.where(lane >= SIDE - EDGE, pltpu.roll(left, (SIDE - EDGE - EDGE * g) % SIDE, 1), 0.0)
        top = g * tall
        count = min(tall, height - top)
        out[top : top + count, :] = part[0:count]


def own_kernel(rows, cols, scalars_in, own, guess, source, compact, scalars):
    fields = PARTS * rows
    scalars[...] = scalars_in[...]
    guess[...] = by_cells(own[0:fields, :], rows)
    source[...] = by_cells(own[fields : 2 * fields, :], rows)
    found = coefficients(*[own[2 * fields + k * rows : 2 * fields + (k + 1) * rows, :] for k in range(3)], scalars_in)
    for k in range(6):
        compact[k] = found[k]


def side_kernel(rows, cols, right, left, before, after, up, down, ends, sems):
    size = right.shape[0]
    copies = []
    for f in range(PARTS):
        copies.append(fetch(before.at[pl.ds((f + 1) * rows - 8, 8)], ends.at[0, f], sems.at[f]))
        copies.append(fetch(after.at[pl.ds(f * rows, 8)], ends.at[1, f], sems.at[PARTS + f]))
    for out in (up, down):
        out[0:size, :] = right[...]
        out[size : 2 * size, :] = left[...]
    for copy in copies:
        copy.wait()
    for out, p, row in ((up, 0, 7), (down, 1, 0)):
        far = jnp.concatenate([ends[p, f, row : row + 1, :] for f in range(PARTS)], axis=0)
        for t in range(cols // SIDE):
            out[2 * size + t * PARTS : 2 * size + (t + 1) * PARTS, :] = far[:, t * SIDE : (t + 1) * SIDE]


def first_kernel(
    rows, cols, scalars, own_guess, own_source, own_compact, before, after, own_side, before_side, after_side, basis_out,
    compact_out, sums, sides, guess, basis, compact, spread, out_sems,
):
    lanes = cols + SIDE
    fields = PARTS * rows
    packed = (before_side, own_side, after_side)
    parts = []
    for p, main in enumerate((before, None, after)):
        unpack_side(packed[p], sides.at[p])
        parts += [(p, 0, main)] if main is not None else []
        parts += [(p, cols, sides.at[p])]
    here = pl.ds(rows, rows)
    guess[pl.ds(rows + 1, rows), :, 0:cols] = own_guess[...]
    basis[0, here, :, 0:cols] = own_source[...]
    compact[:, here, 0:cols] = own_compact[...]
    for p, at, ref in parts:
        size = ref.shape[1]
        guess[pl.ds(1 + p * rows, rows), :, at : at + size] = by_cells(ref[0:fields, :], rows)
        basis[0, pl.ds(p * rows, rows), :, at : at + size] = by_cells(ref[fields : 2 * fields, :], rows)
    shift, pair = [spread_scalar(scalars, i, (PARTS, lanes)) for i in (SHIFT, PAIR)]
    for p, at, ref in parts:
        size = ref.shape[1]
        level = [ref[2 * fields + k * rows : 2 * fields + (k + 1) * rows, :] for k in range(3)]
        found = coefficients(*level, scalars)
        for k in range(6):
            compact[k, p * rows : (p + 1) * rows, at : at + size] = found[k]
    spread_rows(compact, spread, 0, 3 * rows)
    end = before_side.shape[0] - cols // SIDE * PARTS
    for x, p in ((0, 0), (3 * rows + 1, 2)):
        for t in range(cols // SIDE):
            guess[x, :, t * SIDE : (t + 1) * SIDE] = packed[p][end + t * PARTS : end + (t + 1) * PARTS, :]
        guess[x, :, cols:lanes] = jnp.zeros((PARTS, SIDE), jnp.float32)
    half = rows // 2
    outs = [fetch(compact.at[:, pl.ds(half, 2 * rows)], compact_out, out_sems.at[BLOCKS])]

    def start(base, count):
        made = []
        for i in range(count):
            x = base + i
            middle = guess[x + 1]
            applied = scaled_operator(middle, guess[x], guess[x + 2], [spread[k, x] for k in range(6)])
            made.append(basis[0, x] - applied * (1.0 / SCALE) - shift * middle)
        for i in range(count):
            basis[0, base + i] = made[i]

    by_groups(0, 3 * rows, start)
    outs.append(fetch(basis.at[0, pl.ds(half, 2 * rows)], basis_out.at[0], out_sems.at[0]))
    for j in range(POWERS):
        next_block(basis, spread, j, pair * SCALE * SCALE)
        outs.append(fetch(basis.at[j + 1, pl.ds(half, 2 * rows)], basis_out.at[j + 1], out_sems.at[j + 1]))
    tile = packed_gram(basis, rows, rows, cols)
    for i in range(sums.shape[0]):
        sums[i] = tile
    for copy in outs:
        copy.wait()


def second_kernel(
    rows, cols, scalars, tiles, basis_in, compact, guess, basis_out, solution, sums, old, basis, spread, weights, in_sems,
    out_sems,
):
    shift, pair = scalars[SHIFT : SHIFT + 1, :], scalars[PAIR : PAIR + 1, :]
    copies = [fetch(basis_in.at[j], old.at[j], in_sems.at[j]) for j in range(BLOCKS)]
    half = rows // 2
    spread_rows(compact, spread, 0, 2 * rows)
    update, residual = cycles(jnp.sum(tiles[...], axis=0), shift, pair)
    set_weights(weights, 0, residual)
    set_weights(weights, 1, update)
    for copy in copies:
        copy.wait()

    def one(t, _):
        for i in range(4):
            x = 4 * t + i
            basis[0, x] = mixed(weights, 0, [old[j, x] for j in range(BLOCKS)])

    lax.fori_loop(0, 2 * rows // 4, one, None)

    def move(t, _):
        for i in range(4):
            x = 4 * t + i
            solution[x] = guess[x] + mixed(weights, 1, [old[j, half + x, :, 0:cols] for j in range(POWERS)])

    lax.fori_loop(0, rows // 4, move, None)
    pair = spread_scalar(scalars, PAIR, basis.shape[2:])
    outs = []
    inside = (pl.ds(half, rows), slice(None), pl.ds(0, cols))
    outs.append(fetch(basis.at[(0, *inside)], basis_out.at[0], out_sems.at[0]))
    for j in range(POWERS):
        next_block(basis, spread, j, pair * SCALE * SCALE)
        outs.append(fetch(basis.at[(j + 1, *inside)], basis_out.at[j + 1], out_sems.at[j + 1]))
    tile = packed_gram(basis, half, rows, cols)
    for i in range(sums.shape[0]):
        sums[i] = tile
    for copy in outs:
        copy.wait()


def third_kernel(rows, cols, scalars, tiles, old, start, solution, residual, made, weights):
    shift, pair = scalars[SHIFT : SHIFT + 1, :], scalars[PAIR : PAIR + 1, :]
    update, left = cycles(jnp.sum(tiles[...], axis=0), shift, pair)
    set_weights(weights, 0, left)
    set_weights(weights, 1, update)

    def move(t, _):
        for i in range(4):
            x = 4 * t + i
            blocks = [old[j, x] for j in range(BLOCKS)]
            made[0, x] = mixed(weights, 0, blocks)
            made[1, x] = start[x] + mixed(weights, 1, blocks[:POWERS])

    lax.fori_loop(0, rows // 4, move, None)
    residual[...] = by_fields(made[0])
    solution[...] = by_fields(made[1])


def summed(copies):
    got = lax.all_to_all(copies, "lat", 0, 0, tiled=True)
    near = jnp.sum(got, axis=0)
    sent = jnp.broadcast_to(near[None], (lax.axis_size("dep"),) + near.shape)
    return lax.all_to_all(sent, "dep", 0, 0, tiled=True)


def shards(x_start, source, eps_table, labels, pml_level):
    rows, cols = labels.shape
    lanes = cols + SIDE
    f32 = jnp.float32
    vmem = pl.BlockSpec(memory_space=pltpu.VMEM)
    anywhere = pl.BlockSpec(memory_space=pl.ANY)
    hbm = pl.BlockSpec(memory_space=pltpu.HBM)

    def params(mib):
        return pltpu.CompilerParams(vmem_limit_bytes=mib * MIB)

    lat_size = lax.axis_size("lat")
    start = x_start.reshape(PARTS * rows, cols)
    height = (2 * PARTS + 3) * rows
    count = PARTS * rows
    dma = pltpu.SemaphoreType.DMA
    tall = packed_rows(height)
    fields, first, last, scalars = pl.pallas_call(
        functools.partial(pack_kernel, rows, cols),
        out_shape=[
            jax.ShapeDtypeStruct((height, cols), f32),
            jax.ShapeDtypeStruct((tall, SIDE), f32),
            jax.ShapeDtypeStruct((tall, SIDE), f32),
            jax.ShapeDtypeStruct((3 * LABELS, SIDE), f32),
        ],
        in_specs=[hbm] * 5,
        out_specs=[vmem] * 4,
        scratch_shapes=[pltpu.SMEM(eps_table.shape, f32), pltpu.VMEM((3 * rows, cols), jnp.int32), dma((5,))],
        compiler_params=params(56),
        name="pack",
    )(eps_table, start, source.reshape(count, cols), labels, pml_level.reshape(2 * rows, cols))

    def along(array, axis, step):
        size = lax.axis_size(axis)
        return lax.ppermute(array, axis, [(i, i + step) for i in range(size) if 0 <= i + step < size])

    before, after = along(fields, "lat", 1), along(fields, "lat", -1)
    right, left = along(first, "dep", -1), along(last, "dep", 1)
    guess, seen, own_compact, scalars = pl.pallas_call(
        functools.partial(own_kernel, rows, cols),
        out_shape=[
            jax.ShapeDtypeStruct((rows, PARTS, cols), f32),
            jax.ShapeDtypeStruct((rows, PARTS, cols), f32),
            jax.ShapeDtypeStruct((6, rows, cols), f32),
            jax.ShapeDtypeStruct(scalars.shape, f32),
        ],
        in_specs=[vmem] * 2,
        out_specs=[vmem] * 4,
        compiler_params=params(8),
        name="own",
    )(scalars, fields)
    right, left, scalars = lax.optimization_barrier((right, left, scalars))
    both = 2 * tall + cols // SIDE * PARTS
    up, down = pl.pallas_call(
        functools.partial(side_kernel, rows, cols),
        out_shape=[jax.ShapeDtypeStruct((both, SIDE), f32)] * 2,
        in_specs=[vmem, vmem, anywhere, anywhere],
        out_specs=[vmem] * 2,
        scratch_shapes=[pltpu.VMEM((2, PARTS, 8, cols), f32), dma((2 * PARTS,))],
        compiler_params=params(4),
        name="side",
    )(right, left, before, after)
    before_side, after_side = along(up, "lat", 1), along(down, "lat", -1)

    basis, compact, sums = pl.pallas_call(
        functools.partial(first_kernel, rows, cols),
        out_shape=[
            jax.ShapeDtypeStruct((BLOCKS, 2 * rows, PARTS, lanes), f32),
            jax.ShapeDtypeStruct((6, 2 * rows, lanes), f32),
            jax.ShapeDtypeStruct((lat_size, PARTS, SIDE), f32),
        ],
        in_specs=[vmem] * 9,
        out_specs=[hbm, anywhere, vmem],
        scratch_shapes=[
            pltpu.VMEM((3, height, SIDE), f32),
            pltpu.VMEM((3 * rows + 2, PARTS, lanes), f32),
            pltpu.VMEM((BLOCKS, 3 * rows, PARTS, lanes), f32),
            pltpu.VMEM((6, 3 * rows, lanes), f32),
            pltpu.VMEM((6, 3 * rows, PARTS, lanes), f32),
            dma((BLOCKS + 1,)),
        ],
        compiler_params=params(48),
        name="first",
    )(scalars, guess, seen, own_compact, before, after, up, before_side, after_side)
    tiles = summed(sums)
    basis, solution, sums = pl.pallas_call(
        functools.partial(second_kernel, rows, cols),
        out_shape=[
            jax.ShapeDtypeStruct((BLOCKS, rows, PARTS, cols), f32),
            jax.ShapeDtypeStruct((rows, PARTS, cols), f32),
            jax.ShapeDtypeStruct((lat_size, PARTS, SIDE), f32),
        ],
        in_specs=[vmem, vmem, hbm, vmem, vmem],
        out_specs=[anywhere, vmem, vmem],
        scratch_shapes=[
            pltpu.VMEM((BLOCKS, 2 * rows, PARTS, lanes), f32),
            pltpu.VMEM((BLOCKS, 2 * rows, PARTS, lanes), f32),
            pltpu.VMEM((6, 2 * rows, PARTS, lanes), f32),
            pltpu.VMEM((2, ANGLES, BLOCKS, PARTS, SIDE), f32),
            dma((BLOCKS,)),
            dma((BLOCKS,)),
        ],
        compiler_params=params(48),
        name="second",
    )(scalars, tiles, basis, compact, guess)
    tiles = summed(sums)
    solution, residual = pl.pallas_call(
        functools.partial(third_kernel, rows, cols),
        out_shape=[jax.ShapeDtypeStruct((count, cols), f32)] * 2,
        in_specs=[vmem] * 4,
        out_specs=[vmem] * 2,
        scratch_shapes=[
            pltpu.VMEM((2, rows, PARTS, cols), f32),
            pltpu.VMEM((2, ANGLES, BLOCKS, PARTS, SIDE), f32),
        ],
        compiler_params=params(8),
        name="third",
    )(scalars, tiles, basis, solution)
    return solution.reshape(x_start.shape), residual.reshape(x_start.shape)


def solution(mesh):
    in_specs = (
        P(None, None, "lat", "dep"),
        P(None, None, "lat", "dep"),
        P(),
        P("lat", "dep"),
        P(None, "lat", "dep"),
    )
    out_specs = (P(None, None, "lat", "dep"), P(None, None, "lat", "dep"))
    return jax.shard_map(shards, mesh=mesh, in_specs=in_specs, out_specs=out_specs, check_vma=False)
```

```python
import functools

import jax
import jax.numpy as jnp
from jax import lax
from jax.experimental import pallas as pl
from jax.experimental.pallas import tpu as pltpu
from jax.sharding import PartitionSpec as P

S = 4
OUTER = 4
LABELS = 8
PML = 16
ANGLES = 4

sigma_peak = 4.0
k_squared = 2.0

FUSE = 2
POWERS = S * FUSE
BLOCKS = POWERS + 1
PARTS = 2 * ANGLES
HEIGHT = BLOCKS * PARTS
SCALE = 1.5
HIGH = lax.Precision.HIGHEST
SIDE = 128
EDGE = 18
TIERS = SIDE // EDGE
GROUP = 24
MIB = 1024 * 1024


def shifts_of(table):
    real, imag = [sum(table[part, k] for k in range(LABELS)) * (1.0 / LABELS) for part in range(2)]
    root = 0.25 * imag + 0.12
    return 1.25 - 0.25 * real, root * root


def dot(a, b, dims):
    return lax.dot_general(a, b, (dims, ((), ())), precision=HIGH, preferred_element_type=jnp.float32)


def iota(shape, dim):
    return lax.broadcasted_iota(jnp.int32, shape, dim)


def spread_scalar(scalars, i, shape):
    return jnp.concatenate([jnp.broadcast_to(scalars[i : i + 1, :], (shape[0], SIDE))] * (shape[1] // SIDE), axis=1)


SHIFT, PAIR = 2 * LABELS, 2 * LABELS + 1


def coefficients(labels, level_lat, level_dep, scalars):
    eps_real = jnp.zeros_like(labels)
    eps_imag = jnp.zeros_like(labels)
    for k in range(LABELS):
        here = labels == float(k + 1)
        eps_real = jnp.where(here, spread_scalar(scalars, k, labels.shape), eps_real)
        eps_imag = jnp.where(here, spread_scalar(scalars, LABELS + k, labels.shape), eps_imag)

    def stretch_of(level):
        sigma = sigma_peak * (level * (1.0 / PML)) ** 2
        inverse = 1.0 / (1.0 + sigma * sigma)
        return inverse, -sigma * inverse

    lat_real, lat_imag = stretch_of(level_lat)
    dep_real, dep_imag = stretch_of(level_dep)
    centre_real = (lat_real + dep_real) * 0.25 - k_squared / 8.0 * eps_real
    centre_real = centre_real + (1.0 - spread_scalar(scalars, SHIFT, labels.shape))
    centre_imag = (lat_imag + dep_imag) * 0.25 - k_squared / 8.0 * eps_imag
    side = -0.125 * SCALE
    found = (
        SCALE * centre_real,
        side * lat_real,
        side * dep_real,
        SCALE * centre_imag,
        side * lat_imag,
        side * dep_imag,
    )
    return [jnp.where(labels > 0.5, f, 0.0) for f in found]


def by_cells(fields, rows):
    return jnp.swapaxes(fields.reshape(PARTS, rows, fields.shape[1]), 0, 1)


def spread_rows(compact, spread, first, count):
    sign = jnp.where(iota((PARTS, 1), 0) < ANGLES, 1.0, -1.0)

    for x in range(first, first + count):
        for k in range(6):
            line = jnp.broadcast_to(compact[k, x : x + 1, :], spread.shape[2:])
            spread[k, x] = line * sign if k >= 3 else line


def scaled_operator(middle, before, after, factors):
    lanes = middle.shape[1]
    lat = before + after
    dep = pltpu.roll(middle, 1, 1) + pltpu.roll(middle, lanes - 1, 1)
    straight = factors[0] * middle + factors[1] * lat + factors[2] * dep
    crossed = factors[3] * middle + factors[4] * lat + factors[5] * dep
    return straight + pltpu.roll(crossed, ANGLES, 0)


def by_groups(first, last, some):
    full = (last - first) // GROUP
    lax.fori_loop(0, full, lambda t, _: some(first + t * GROUP, GROUP), None)
    if (last - first) % GROUP:
        some(first + full * GROUP, (last - first) % GROUP)


def next_block(basis, spread, j, pair):
    rows = basis.shape[1]

    def some(base, count):
        made = []
        for i in range(count):
            x = base + i
            new = scaled_operator(
                basis[j, x], basis[j, x - 1], basis[j, x + 1], [spread[k, x] for k in range(6)]
            )
            if j % 2 == 1:
                new = new + pair * basis[j - 1, x]
            made.append(new)
        for i in range(count):
            basis[j + 1, base + i] = made[i]

    by_groups(j + 1, rows - 1 - j, some)


def packed_gram(basis, first, rows, cols):
    full = jnp.zeros((HEIGHT, HEIGHT), jnp.float32)
    for x in range(rows):
        block = basis[:, first + x, :, 0:cols].reshape(HEIGHT, cols)
        full = full + dot(block, block, ((1,), (1,)))
    full = jnp.concatenate([full, jnp.zeros((HEIGHT, SIDE - HEIGHT), jnp.float32)], axis=1)
    both = full + pltpu.roll(pltpu.roll(full, SIDE - ANGLES, 1), HEIGHT - ANGLES, 0)
    tile = jnp.zeros((PARTS, SIDE), jnp.float32)
    for j in range(BLOCKS):
        low, move = PLACES[j]
        upper = jnp.where(upper_lanes(j), both[PARTS * j : PARTS * (j + 1)], 0.0)
        upper = pltpu.roll(upper, move % SIDE, 1) if move else upper
        tile = tile + (pltpu.roll(upper, ANGLES, 0) if low else upper)
    return tile


PLACES = {
    0: (False, 0),
    3: (False, 72 - 24),
    8: (False, 120 - 64),
    1: (False, 0 - 8 + ANGLES),
    2: (False, 64 - 16 + ANGLES),
    4: (True, 0 - 32),
    5: (True, 40 - 40),
    6: (True, 72 - 48),
    7: (True, 96 - 56),
}


def upper_lanes(j):
    row, lane = iota((PARTS, SIDE), 0), iota((PARTS, SIDE), 1)
    return (row < ANGLES) & (lane % PARTS < ANGLES) & (lane >= PARTS * j) & (lane < HEIGHT)


def half_gram(tile):
    lane = iota((PARTS, SIDE), 1)
    parts = []
    for j in range(BLOCKS):
        low, move = PLACES[j]
        back = pltpu.roll(tile, ANGLES, 0) if low else tile
        back = pltpu.roll(back, -move % SIDE, 1) if move else back
        weight = jnp.where(lane < PARTS * (j + 1), 0.5, 1.0)
        parts.append(jnp.where(upper_lanes(j), back * weight, 0.0))
    return jnp.concatenate(parts, axis=0)


def solve_normal(gram):
    size = S * ANGLES
    work = gram[0:24]
    work = pltpu.roll(work, 24 - ANGLES, 0)[0:size]
    row, lane = iota((size, SIDE), 0), iota((size, SIDE), 1)
    diagonal = jnp.sum(jnp.where(lane == row + ANGLES, work, 0.0), axis=1, keepdims=True)
    scale = lax.rsqrt(jnp.broadcast_to(diagonal, (size, SIDE)))
    left = [jnp.broadcast_to(work[:, i : i + 1], (size, SIDE)) for i in range(ANGLES, ANGLES + size)]
    left = [column * scale * scale[i : i + 1] for i, column in enumerate(left)] + [work * scale]
    for k in range(0, size, 2):
        one, two = left[0], left[1]
        a, b, c, d = one[k : k + 1], two[k : k + 1], one[k + 1 : k + 2], two[k + 1 : k + 2]
        inverse = 1.0 / (a * d - b * c)
        a, b, c, d = a * inverse, b * inverse, c * inverse, d * inverse
        one, two = one - jnp.where(row == k, 1.0, 0.0), two - jnp.where(row == k + 1, 1.0, 0.0)
        after = []
        for column in left[2:]:
            upper, lower = column[k : k + 1], column[k + 1 : k + 2]
            after.append(column - one * (d * upper - b * lower) - two * (a * lower - c * upper))
        left = after
    return jnp.where(lane < ANGLES, left[0] * scale, 0.0)


def cycles(tile, shift, pair):
    upper = half_gram(tile)
    row, lane = iota((HEIGHT, SIDE), 0), iota((HEIGHT, SIDE), 1)
    even = jnp.where(((row // PARTS) % 2 == 0) & (row < HEIGHT - PARTS), pair * SCALE, 0.0)
    residual = jnp.where((row == lane) & (lane < ANGLES), 1.0, 0.0)
    update = jnp.zeros((HEIGHT, SIDE), jnp.float32)
    blank = jnp.zeros((SIDE - HEIGHT, SIDE), jnp.float32)
    for cycle in range(FUSE):
        power = residual
        powers = residual
        for k in range(1, S + 1):
            power = (
                pltpu.roll(power, PARTS, 0) * (1.0 / SCALE)
                + power * shift
                - pltpu.roll(power, HEIGHT - PARTS, 0) * even
            )
            powers = powers + pltpu.roll(power, ANGLES * k, 1)
        half = dot(upper, jnp.concatenate([powers, blank], axis=0), ((1,), (0,)))
        gram = dot(powers, half, ((0,), (0,))) + dot(half, powers, ((0,), (0,)))
        shifted = pltpu.roll(powers, SIDE - ANGLES, 1)
        mixing = solve_normal(gram)
        mixing = jnp.concatenate([mixing, jnp.zeros((SIDE - S * ANGLES, SIDE), jnp.float32)], axis=0)
        update = update + dot(powers, mixing, ((1,), (0,)))
        residual = residual - dot(shifted, mixing, ((1,), (0,)))
    return update, residual


def set_weights(weights, which, table):
    row, lane = iota((HEIGHT, SIDE), 0), iota((HEIGHT, SIDE), 1)
    for d in range(ANGLES):
        picked = jnp.where(lane == (row - d + ANGLES) % ANGLES, table, 0.0)
        picked = jnp.broadcast_to(jnp.sum(picked, axis=1, keepdims=True), (HEIGHT, SIDE))
        for j in range(BLOCKS):
            single = picked[PARTS * j : PARTS * (j + 1)]
            weights[which, d, j] = single + pltpu.roll(single, ANGLES, 0)


def mixed(weights, which, blocks):
    lanes = blocks[0].shape[1]
    angle = iota((PARTS, lanes), 0) % ANGLES
    total = None
    for d in range(ANGLES):
        turned = None
        for j, block in enumerate(blocks):
            factor = weights[which, d, j]
            term = jnp.concatenate([factor] * (lanes // SIDE), axis=1) * block
            turned = term if turned is None else turned + term
        if d:
            turned = jnp.where(
                angle + d < ANGLES, pltpu.roll(turned, PARTS - d, 0), pltpu.roll(turned, ANGLES - d, 0)
            )
        total = turned if total is None else total + turned
    return total


def fetch(source, target, sem):
    copy = pltpu.make_async_copy(source, target, sem)
    copy.start()
    return copy


def packed_rows(height):
    return -(-height // (TIERS * 8)) * 8


def pack_kernel(rows, cols, table_in, start, source, labels, levels, fields_out, first, last, scalars, fields, table, marks, sems):
    size = PARTS * rows
    height = fields.shape[0]
    copies = [
        fetch(labels, marks.at[pl.ds(0, rows)], sems.at[0]),
        fetch(levels, marks.at[pl.ds(rows, 2 * rows)], sems.at[1]),
        fetch(start, fields.at[pl.ds(0, size)], sems.at[2]),
        fetch(source, fields.at[pl.ds(size, size)], sems.at[3]),
        fetch(table_in, table, sems.at[4]),
    ]
    outs = []

    def send(at, count):
        outs.append(fetch(fields.at[pl.ds(at, count)], fields_out.at[pl.ds(at, count)], sems.at[5 + len(outs)]))

    copies[0].wait()
    copies[1].wait()
    fields[2 * size : 2 * size + rows, :] = (marks[0:rows, :] + 1).astype(jnp.float32)
    fields[2 * size + rows : height, :] = marks[rows:, :].astype(jnp.float32)
    send(2 * size, 3 * rows)
    copies[2].wait()
    send(0, size)
    copies[3].wait()
    send(size, size)
    copies[4].wait()
    row = iota(scalars.shape, 0)
    known = jnp.zeros(scalars.shape, jnp.float32)
    for i, value in enumerate([table[p, k] for p in range(2) for k in range(LABELS)] + list(shifts_of(table))):
        known = jnp.where(row == i, value, known)
    scalars[...] = known
    tall = packed_rows(height)
    lane = iota((tall, SIDE), 1)
    for out, at, keep, origin in ((first, 0, lane < EDGE, 0), (last, cols - SIDE, lane >= SIDE - EDGE, SIDE - EDGE)):
        total = jnp.zeros((tall, SIDE), jnp.float32)
        for g in range(TIERS):
            top = g * tall
            part = fields[top : min(top + tall, height), at : at + SIDE]
            if part.shape[0] < tall:
                part = jnp.concatenate([part, jnp.zeros((tall - part.shape[0], SIDE), jnp.float32)], axis=0)
            total = total + pltpu.roll(jnp.where(keep, part, 0.0), (EDGE * g - origin) % SIDE, 1)
        out[...] = total
    for copy in outs:
        copy.wait()


def unpack_side(packed, out):
    height = out.shape[0]
    tall = packed_rows(height)
    lane = iota((tall, SIDE), 1)
    right, left = packed[0:tall, :], packed[tall : 2 * tall, :]
    for g in range(TIERS):
        part = jnp.where(lane < EDGE, pltpu.roll(right, -EDGE * g % SIDE, 1), 0.0)
        part = part + jnp.where(lane >= SIDE - EDGE, pltpu.roll(left, (SIDE - EDGE - EDGE * g) % SIDE, 1), 0.0)
        top = g * tall
        count = min(tall, height - top)
        out[top : top + count, :] = part[0:count]


def own_kernel(rows, cols, scalars_in, own, guess, source, compact, scalars):
    fields = PARTS * rows
    scalars[...] = scalars_in[...]
    guess[...] = by_cells(own[0:fields, :], rows)
    source[...] = by_cells(own[fields : 2 * fields, :], rows)
    found = coefficients(*[own[2 * fields + k * rows : 2 * fields + (k + 1) * rows, :] for k in range(3)], scalars_in)
    for k in range(6):
        compact[k] = found[k]


def side_kernel(rows, cols, right, left, before, after, up, down, ends, sems):
    size = right.shape[0]
    copies = []
    for f in range(PARTS):
        copies.append(fetch(before.at[pl.ds((f + 1) * rows - 8, 8)], ends.at[0, f], sems.at[f]))
        copies.append(fetch(after.at[pl.ds(f * rows, 8)], ends.at[1, f], sems.at[PARTS + f]))
    for out in (up, down):
        out[0:size, :] = right[...]
        out[size : 2 * size, :] = left[...]
    for copy in copies:
        copy.wait()
    for out, p, row in ((up, 0, 7), (down, 1, 0)):
        far = jnp.concatenate([ends[p, f, row : row + 1, :] for f in range(PARTS)], axis=0)
        for t in range(cols // SIDE):
            out[2 * size + t * PARTS : 2 * size + (t + 1) * PARTS, :] = far[:, t * SIDE : (t + 1) * SIDE]


def first_kernel(
    rows, cols, scalars, own_guess, own_source, own_compact, before, after, own_side, before_side, after_side, basis_out,
    compact_out, sums, sides, guess, basis, compact, spread, out_sems,
):
    lanes = cols + SIDE
    fields = PARTS * rows
    packed = (before_side, own_side, after_side)
    parts = []
    for p, main in enumerate((before, None, after)):
        unpack_side(packed[p], sides.at[p])
        parts += [(p, 0, main)] if main is not None else []
        parts += [(p, cols, sides.at[p])]
    here = pl.ds(rows, rows)
    guess[pl.ds(rows + 1, rows), :, 0:cols] = own_guess[...]
    basis[0, here, :, 0:cols] = own_source[...]
    compact[:, here, 0:cols] = own_compact[...]
    for p, at, ref in parts:
        size = ref.shape[1]
        guess[pl.ds(1 + p * rows, rows), :, at : at + size] = by_cells(ref[0:fields, :], rows)
        basis[0, pl.ds(p * rows, rows), :, at : at + size] = by_cells(ref[fields : 2 * fields, :], rows)
    shift, pair = [spread_scalar(scalars, i, (PARTS, lanes)) for i in (SHIFT, PAIR)]
    for p, at, ref in parts:
        size = ref.shape[1]
        level = [ref[2 * fields + k * rows : 2 * fields + (k + 1) * rows, :] for k in range(3)]
        found = coefficients(*level, scalars)
        for k in range(6):
            compact[k, p * rows : (p + 1) * rows, at : at + size] = found[k]
    spread_rows(compact, spread, 0, 3 * rows)
    end = before_side.shape[0] - cols // SIDE * PARTS
    for x, p in ((0, 0), (3 * rows + 1, 2)):
        for t in range(cols // SIDE):
            guess[x, :, t * SIDE : (t + 1) * SIDE] = packed[p][end + t * PARTS : end + (t + 1) * PARTS, :]
        guess[x, :, cols:lanes] = jnp.zeros((PARTS, SIDE), jnp.float32)
    half = rows // 2
    compact_out[...] = compact[:, half : half + 2 * rows, :]
    outs = []

    def start(base, count):
        made = []
        for i in range(count):
            x = base + i
            middle = guess[x + 1]
            applied = scaled_operator(middle, guess[x], guess[x + 2], [spread[k, x] for k in range(6)])
            made.append(basis[0, x] - applied * (1.0 / SCALE) - shift * middle)
        for i in range(count):
            basis[0, base + i] = made[i]

    by_groups(0, 3 * rows, start)
    outs.append(fetch(basis.at[0, pl.ds(half, 2 * rows)], basis_out.at[0], out_sems.at[0]))
    for j in range(POWERS):
        next_block(basis, spread, j, pair * SCALE * SCALE)
        outs.append(fetch(basis.at[j + 1, pl.ds(half, 2 * rows)], basis_out.at[j + 1], out_sems.at[j + 1]))
    tile = packed_gram(basis, rows, rows, cols)
    for i in range(sums.shape[0]):
        sums[i] = tile
    for copy in outs:
        copy.wait()


def second_kernel(
    rows, cols, scalars, tiles, basis_in, compact, guess, basis_out, solution, sums, old, basis, spread, weights, in_sems,
):
    shift, pair = scalars[SHIFT : SHIFT + 1, :], scalars[PAIR : PAIR + 1, :]
    copies = [fetch(basis_in.at[j], old.at[j], in_sems.at[j]) for j in range(BLOCKS)]
    half = rows // 2
    spread_rows(compact, spread, 0, 2 * rows)
    update, residual = cycles(jnp.sum(tiles[...], axis=0), shift, pair)
    set_weights(weights, 0, residual)
    set_weights(weights, 1, update)
    for copy in copies:
        copy.wait()

    def one(t, _):
        for i in range(4):
            x = 4 * t + i
            basis[0, x] = mixed(weights, 0, [old[j, x] for j in range(BLOCKS)])

    lax.fori_loop(0, 2 * rows // 4, one, None)

    def move(t, _):
        for i in range(4):
            x = 4 * t + i
            solution[x] = guess[x] + mixed(weights, 1, [old[j, half + x, :, 0:cols] for j in range(POWERS)])

    lax.fori_loop(0, rows // 4, move, None)
    pair = spread_scalar(scalars, PAIR, basis.shape[2:])
    for j in range(POWERS):
        next_block(basis, spread, j, pair * SCALE * SCALE)
    basis_out[...] = basis[:, half : half + rows, :, 0:cols]
    tile = packed_gram(basis, half, rows, cols)
    for i in range(sums.shape[0]):
        sums[i] = tile


def third_kernel(rows, cols, scalars, tiles, old, start, solution, residual, made, turned, weights, sems):
    shift, pair = scalars[SHIFT : SHIFT + 1, :], scalars[PAIR : PAIR + 1, :]
    update, left = cycles(jnp.sum(tiles[...], axis=0), shift, pair)
    set_weights(weights, 0, left)
    set_weights(weights, 1, update)

    def move(t, _):
        for i in range(4):
            x = 4 * t + i
            blocks = [old[j, x] for j in range(BLOCKS)]
            made[0, x] = mixed(weights, 0, blocks)
            made[1, x] = start[x] + mixed(weights, 1, blocks[:POWERS])

    outs = []
    for half in range(2):
        count = rows // 2
        top = half * count
        lax.fori_loop(top // 4, (top + count) // 4, move, None)
        for k, out in enumerate((residual, solution)):
            turned[k, half] = jnp.swapaxes(made[k, top : top + count], 0, 1)
            outs.append(fetch(turned.at[k, half], out.at[:, pl.ds(top, count)], sems.at[k, half]))
    for copy in outs:
        copy.wait()


def summed(copies):
    got = lax.all_to_all(copies, "lat", 0, 0, tiled=True)
    near = jnp.sum(got, axis=0)
    sent = jnp.broadcast_to(near[None], (lax.axis_size("dep"),) + near.shape)
    return lax.all_to_all(sent, "dep", 0, 0, tiled=True)


def shards(x_start, source, eps_table, labels, pml_level):
    rows, cols = labels.shape
    lanes = cols + SIDE
    f32 = jnp.float32
    vmem = pl.BlockSpec(memory_space=pltpu.VMEM)
    anywhere = pl.BlockSpec(memory_space=pl.ANY)
    hbm = pl.BlockSpec(memory_space=pltpu.HBM)

    def params(mib):
        return pltpu.CompilerParams(vmem_limit_bytes=mib * MIB)

    lat_size = lax.axis_size("lat")
    start = x_start.reshape(PARTS * rows, cols)
    height = (2 * PARTS + 3) * rows
    count = PARTS * rows
    dma = pltpu.SemaphoreType.DMA
    tall = packed_rows(height)
    fields, first, last, scalars = pl.pallas_call(
        functools.partial(pack_kernel, rows, cols),
        out_shape=[
            jax.ShapeDtypeStruct((height, cols), f32),
            jax.ShapeDtypeStruct((tall, SIDE), f32),
            jax.ShapeDtypeStruct((tall, SIDE), f32),
            jax.ShapeDtypeStruct((3 * LABELS, SIDE), f32),
        ],
        in_specs=[hbm] * 5,
        out_specs=[hbm] + [vmem] * 3,
        scratch_shapes=[
            pltpu.VMEM((height, cols), f32),
            pltpu.SMEM(eps_table.shape, f32),
            pltpu.VMEM((3 * rows, cols), jnp.int32),
            dma((8,)),
        ],
        compiler_params=params(56),
        name="pack",
    )(eps_table, start, source.reshape(count, cols), labels, pml_level.reshape(2 * rows, cols))

    def along(array, axis, step):
        size = lax.axis_size(axis)
        return lax.ppermute(array, axis, [(i, i + step) for i in range(size) if 0 <= i + step < size])

    before, after = along(fields, "lat", 1), along(fields, "lat", -1)
    right, left = along(first, "dep", -1), along(last, "dep", 1)
    guess, seen, own_compact, scalars = pl.pallas_call(
        functools.partial(own_kernel, rows, cols),
        out_shape=[
            jax.ShapeDtypeStruct((rows, PARTS, cols), f32),
            jax.ShapeDtypeStruct((rows, PARTS, cols), f32),
            jax.ShapeDtypeStruct((6, rows, cols), f32),
            jax.ShapeDtypeStruct(scalars.shape, f32),
        ],
        in_specs=[vmem] * 2,
        out_specs=[vmem] * 4,
        compiler_params=params(8),
        name="own",
    )(scalars, fields)
    right, left, scalars = lax.optimization_barrier((right, left, scalars))
    both = 2 * tall + cols // SIDE * PARTS
    up, down = pl.pallas_call(
        functools.partial(side_kernel, rows, cols),
        out_shape=[jax.ShapeDtypeStruct((both, SIDE), f32)] * 2,
        in_specs=[vmem, vmem, anywhere, anywhere],
        out_specs=[vmem] * 2,
        scratch_shapes=[pltpu.VMEM((2, PARTS, 8, cols), f32), dma((2 * PARTS,))],
        compiler_params=params(4),
        name="side",
    )(right, left, before, after)
    before_side, after_side = along(up, "lat", 1), along(down, "lat", -1)

    basis, compact, sums = pl.pallas_call(
        functools.partial(first_kernel, rows, cols),
        out_shape=[
            jax.ShapeDtypeStruct((BLOCKS, 2 * rows, PARTS, lanes), f32),
            jax.ShapeDtypeStruct((6, 2 * rows, lanes), f32),
            jax.ShapeDtypeStruct((lat_size, PARTS, SIDE), f32),
        ],
        in_specs=[vmem] * 9,
        out_specs=[hbm, vmem, vmem],
        scratch_shapes=[
            pltpu.VMEM((3, height, SIDE), f32),
            pltpu.VMEM((3 * rows + 2, PARTS, lanes), f32),
            pltpu.VMEM((BLOCKS, 3 * rows, PARTS, lanes), f32),
            pltpu.VMEM((6, 3 * rows, lanes), f32),
            pltpu.VMEM((6, 3 * rows, PARTS, lanes), f32),
            dma((BLOCKS,)),
        ],
        compiler_params=params(48),
        name="first",
    )(scalars, guess, seen, own_compact, before, after, up, before_side, after_side)
    tiles = summed(sums)
    basis, solution, sums = pl.pallas_call(
        functools.partial(second_kernel, rows, cols),
        out_shape=[
            jax.ShapeDtypeStruct((BLOCKS, rows, PARTS, cols), f32),
            jax.ShapeDtypeStruct((rows, PARTS, cols), f32),
            jax.ShapeDtypeStruct((lat_size, PARTS, SIDE), f32),
        ],
        in_specs=[vmem, vmem, hbm, vmem, vmem],
        out_specs=[vmem, vmem, vmem],
        scratch_shapes=[
            pltpu.VMEM((BLOCKS, 2 * rows, PARTS, lanes), f32),
            pltpu.VMEM((BLOCKS, 2 * rows, PARTS, lanes), f32),
            pltpu.VMEM((6, 2 * rows, PARTS, lanes), f32),
            pltpu.VMEM((2, ANGLES, BLOCKS, PARTS, SIDE), f32),
            dma((BLOCKS,)),
        ],
        compiler_params=params(48),
        name="second",
    )(scalars, tiles, basis, compact, guess)
    tiles = summed(sums)
    solution, residual = pl.pallas_call(
        functools.partial(third_kernel, rows, cols),
        out_shape=[jax.ShapeDtypeStruct((PARTS, rows, cols), f32)] * 2,
        in_specs=[vmem] * 4,
        out_specs=[hbm] * 2,
        scratch_shapes=[
            pltpu.VMEM((2, rows, PARTS, cols), f32),
            pltpu.VMEM((2, 2, PARTS, rows // 2, cols), f32),
            pltpu.VMEM((2, ANGLES, BLOCKS, PARTS, SIDE), f32),
            dma((2, 2)),
        ],
        compiler_params=params(8),
        name="third",
    )(scalars, tiles, basis, solution)
    return solution.reshape(x_start.shape), residual.reshape(x_start.shape)


def solution(mesh):
    in_specs = (
        P(None, None, "lat", "dep"),
        P(None, None, "lat", "dep"),
        P(),
        P("lat", "dep"),
        P(None, "lat", "dep"),
    )
    out_specs = (P(None, None, "lat", "dep"), P(None, None, "lat", "dep"))
    return jax.shard_map(shards, mesh=mesh, in_specs=in_specs, out_specs=out_specs, check_vma=False)
```

```python
import functools

import jax
import jax.numpy as jnp
from jax import lax
from jax.experimental import pallas as pl
from jax.experimental.pallas import tpu as pltpu
from jax.sharding import PartitionSpec as P

S = 4
OUTER = 4
LABELS = 8
PML = 16
ANGLES = 4

sigma_peak = 4.0
k_squared = 2.0

FUSE = 2
POWERS = S * FUSE
BLOCKS = POWERS + 1
PARTS = 2 * ANGLES
HEIGHT = BLOCKS * PARTS
SCALE = 1.5
HIGH = lax.Precision.HIGHEST
SIDE = 128
EDGE = 18
TIERS = SIDE // EDGE
KEPT = 4
GROUP = 24
MIB = 1024 * 1024


def shifts_of(table):
    real, imag = [sum(table[part, k] for k in range(LABELS)) * (1.0 / LABELS) for part in range(2)]
    root = 0.25 * imag + 0.12
    return 1.25 - 0.25 * real, root * root


def dot(a, b, dims):
    return lax.dot_general(a, b, (dims, ((), ())), precision=HIGH, preferred_element_type=jnp.float32)


def iota(shape, dim):
    return lax.broadcasted_iota(jnp.int32, shape, dim)


def spread_scalar(scalars, i, shape):
    return jnp.concatenate([jnp.broadcast_to(scalars[i : i + 1, :], (shape[0], SIDE))] * (shape[1] // SIDE), axis=1)


SHIFT, PAIR = 2 * LABELS, 2 * LABELS + 1


def coefficients(labels, level_lat, level_dep, scalars):
    eps_real = jnp.zeros_like(labels)
    eps_imag = jnp.zeros_like(labels)
    for k in range(LABELS):
        here = labels == float(k + 1)
        eps_real = jnp.where(here, spread_scalar(scalars, k, labels.shape), eps_real)
        eps_imag = jnp.where(here, spread_scalar(scalars, LABELS + k, labels.shape), eps_imag)

    def stretch_of(level):
        sigma = sigma_peak * (level * (1.0 / PML)) ** 2
        inverse = 1.0 / (1.0 + sigma * sigma)
        return inverse, -sigma * inverse

    lat_real, lat_imag = stretch_of(level_lat)
    dep_real, dep_imag = stretch_of(level_dep)
    centre_real = (lat_real + dep_real) * 0.25 - k_squared / 8.0 * eps_real
    centre_real = centre_real + (1.0 - spread_scalar(scalars, SHIFT, labels.shape))
    centre_imag = (lat_imag + dep_imag) * 0.25 - k_squared / 8.0 * eps_imag
    side = -0.125 * SCALE
    found = (
        SCALE * centre_real,
        side * lat_real,
        side * dep_real,
        SCALE * centre_imag,
        side * lat_imag,
        side * dep_imag,
    )
    return [jnp.where(labels > 0.5, f, 0.0) for f in found]


def by_cells(fields, rows):
    return jnp.swapaxes(fields.reshape(PARTS, rows, fields.shape[1]), 0, 1)


def spread_rows(compact, spread, first, count):
    sign = jnp.where(iota((PARTS, 1), 0) < ANGLES, 1.0, -1.0)

    for x in range(first, first + count):
        for k in range(6):
            line = jnp.broadcast_to(compact[k, x : x + 1, :], spread.shape[2:])
            spread[k, x] = line * sign if k >= 3 else line


def scaled_operator(middle, before, after, factors):
    lanes = middle.shape[1]
    lat = before + after
    dep = pltpu.roll(middle, 1, 1) + pltpu.roll(middle, lanes - 1, 1)
    straight = factors[0] * middle + factors[1] * lat + factors[2] * dep
    crossed = factors[3] * middle + factors[4] * lat + factors[5] * dep
    return straight + pltpu.roll(crossed, ANGLES, 0)


def by_groups(first, last, some):
    full = (last - first) // GROUP
    lax.fori_loop(0, full, lambda t, _: some(first + t * GROUP, GROUP), None)
    if (last - first) % GROUP:
        some(first + full * GROUP, (last - first) % GROUP)


def next_block(basis, spread, j, pair):
    rows = basis.shape[1]

    def some(base, count):
        made = []
        for i in range(count):
            x = base + i
            new = scaled_operator(
                basis[j, x], basis[j, x - 1], basis[j, x + 1], [spread[k, x] for k in range(6)]
            )
            if j % 2 == 1:
                new = new + pair * basis[j - 1, x]
            made.append(new)
        for i in range(count):
            basis[j + 1, base + i] = made[i]

    by_groups(j + 1, rows - 1 - j, some)


def packed_gram(basis, first, rows, cols):
    full = jnp.zeros((HEIGHT, HEIGHT), jnp.float32)
    for x in range(rows):
        block = basis[:, first + x, :, 0:cols].reshape(HEIGHT, cols)
        full = full + dot(block, block, ((1,), (1,)))
    full = jnp.concatenate([full, jnp.zeros((HEIGHT, SIDE - HEIGHT), jnp.float32)], axis=1)
    both = full + pltpu.roll(pltpu.roll(full, SIDE - ANGLES, 1), HEIGHT - ANGLES, 0)
    tile = jnp.zeros((PARTS, SIDE), jnp.float32)
    for j in range(BLOCKS):
        low, move = PLACES[j]
        upper = jnp.where(upper_lanes(j), both[PARTS * j : PARTS * (j + 1)], 0.0)
        upper = pltpu.roll(upper, move % SIDE, 1) if move else upper
        tile = tile + (pltpu.roll(upper, ANGLES, 0) if low else upper)
    return tile


PLACES = {
    0: (False, 0),
    3: (False, 72 - 24),
    8: (False, 120 - 64),
    1: (False, 0 - 8 + ANGLES),
    2: (False, 64 - 16 + ANGLES),
    4: (True, 0 - 32),
    5: (True, 40 - 40),
    6: (True, 72 - 48),
    7: (True, 96 - 56),
}


def upper_lanes(j):
    row, lane = iota((PARTS, SIDE), 0), iota((PARTS, SIDE), 1)
    return (row < ANGLES) & (lane % PARTS < ANGLES) & (lane >= PARTS * j) & (lane < HEIGHT)


def half_gram(tile):
    lane = iota((PARTS, SIDE), 1)
    parts = []
    for j in range(BLOCKS):
        low, move = PLACES[j]
        back = pltpu.roll(tile, ANGLES, 0) if low else tile
        back = pltpu.roll(back, -move % SIDE, 1) if move else back
        weight = jnp.where(lane < PARTS * (j + 1), 0.5, 1.0)
        parts.append(jnp.where(upper_lanes(j), back * weight, 0.0))
    return jnp.concatenate(parts, axis=0)


def solve_normal(gram):
    size = S * ANGLES
    work = gram[0:24]
    work = pltpu.roll(work, 24 - ANGLES, 0)[0:size]
    row, lane = iota((size, SIDE), 0), iota((size, SIDE), 1)
    diagonal = jnp.sum(jnp.where(lane == row + ANGLES, work, 0.0), axis=1, keepdims=True)
    scale = lax.rsqrt(jnp.broadcast_to(diagonal, (size, SIDE)))
    left = [jnp.broadcast_to(work[:, i : i + 1], (size, SIDE)) for i in range(ANGLES, ANGLES + size)]
    left = [column * scale * scale[i : i + 1] for i, column in enumerate(left)] + [work * scale]
    for k in range(0, size, 2):
        one, two = left[0], left[1]
        a, b, c, d = one[k : k + 1], two[k : k + 1], one[k + 1 : k + 2], two[k + 1 : k + 2]
        inverse = 1.0 / (a * d - b * c)
        a, b, c, d = a * inverse, b * inverse, c * inverse, d * inverse
        one, two = one - jnp.where(row == k, 1.0, 0.0), two - jnp.where(row == k + 1, 1.0, 0.0)
        after = []
        for column in left[2:]:
            upper, lower = column[k : k + 1], column[k + 1 : k + 2]
            after.append(column - one * (d * upper - b * lower) - two * (a * lower - c * upper))
        left = after
    return jnp.where(lane < ANGLES, left[0] * scale, 0.0)


def cycles(tile, shift, pair):
    upper = half_gram(tile)
    row, lane = iota((HEIGHT, SIDE), 0), iota((HEIGHT, SIDE), 1)
    even = jnp.where(((row // PARTS) % 2 == 0) & (row < HEIGHT - PARTS), pair * SCALE, 0.0)
    residual = jnp.where((row == lane) & (lane < ANGLES), 1.0, 0.0)
    update = jnp.zeros((HEIGHT, SIDE), jnp.float32)
    blank = jnp.zeros((SIDE - HEIGHT, SIDE), jnp.float32)
    for cycle in range(FUSE):
        power = residual
        powers = residual
        for k in range(1, S + 1):
            power = (
                pltpu.roll(power, PARTS, 0) * (1.0 / SCALE)
                + power * shift
                - pltpu.roll(power, HEIGHT - PARTS, 0) * even
            )
            powers = powers + pltpu.roll(power, ANGLES * k, 1)
        half = dot(upper, jnp.concatenate([powers, blank], axis=0), ((1,), (0,)))
        gram = dot(powers, half, ((0,), (0,))) + dot(half, powers, ((0,), (0,)))
        shifted = pltpu.roll(powers, SIDE - ANGLES, 1)
        mixing = solve_normal(gram)
        mixing = jnp.concatenate([mixing, jnp.zeros((SIDE - S * ANGLES, SIDE), jnp.float32)], axis=0)
        update = update + dot(powers, mixing, ((1,), (0,)))
        residual = residual - dot(shifted, mixing, ((1,), (0,)))
    return update, residual


def set_weights(weights, which, table):
    row, lane = iota((HEIGHT, SIDE), 0), iota((HEIGHT, SIDE), 1)
    for d in range(ANGLES):
        picked = jnp.where(lane == (row - d + ANGLES) % ANGLES, table, 0.0)
        picked = jnp.broadcast_to(jnp.sum(picked, axis=1, keepdims=True), (HEIGHT, SIDE))
        for j in range(BLOCKS):
            single = picked[PARTS * j : PARTS * (j + 1)]
            weights[which, d, j] = single + pltpu.roll(single, ANGLES, 0)


def mixed(weights, which, blocks):
    lanes = blocks[0].shape[1]
    angle = iota((PARTS, lanes), 0) % ANGLES
    total = None
    for d in range(ANGLES):
        turned = None
        for j, block in enumerate(blocks):
            factor = weights[which, d, j]
            term = jnp.concatenate([factor] * (lanes // SIDE), axis=1) * block
            turned = term if turned is None else turned + term
        if d:
            turned = jnp.where(
                angle + d < ANGLES, pltpu.roll(turned, PARTS - d, 0), pltpu.roll(turned, ANGLES - d, 0)
            )
        total = turned if total is None else total + turned
    return total


def fetch(source, target, sem):
    copy = pltpu.make_async_copy(source, target, sem)
    copy.start()
    return copy


def packed_rows(height):
    return -(-height // (TIERS * 8)) * 8


def pack_kernel(rows, cols, table_in, start, source, labels, levels, fields, first, last, scalars, table, marks, sems):
    size = PARTS * rows
    height = fields.shape[0]
    copies = [
        fetch(labels, marks.at[pl.ds(0, rows)], sems.at[0]),
        fetch(levels, marks.at[pl.ds(rows, 2 * rows)], sems.at[1]),
        fetch(start, fields.at[pl.ds(0, size)], sems.at[2]),
        fetch(source, fields.at[pl.ds(size, size)], sems.at[3]),
        fetch(table_in, table, sems.at[4]),
    ]
    for copy in copies:
        copy.wait()
    fields[2 * size : 2 * size + rows, :] = (marks[0:rows, :] + 1).astype(jnp.float32)
    fields[2 * size + rows : height, :] = marks[rows:, :].astype(jnp.float32)
    row = iota(scalars.shape, 0)
    known = jnp.zeros(scalars.shape, jnp.float32)
    for i, value in enumerate([table[p, k] for p in range(2) for k in range(LABELS)] + list(shifts_of(table))):
        known = jnp.where(row == i, value, known)
    scalars[...] = known
    tall = packed_rows(height)
    lane = iota((tall, SIDE), 1)
    for out, at, keep, origin in ((first, 0, lane < EDGE, 0), (last, cols - SIDE, lane >= SIDE - EDGE, SIDE - EDGE)):
        total = jnp.zeros((tall, SIDE), jnp.float32)
        for g in range(TIERS):
            top = g * tall
            part = fields[top : min(top + tall, height), at : at + SIDE]
            if part.shape[0] < tall:
                part = jnp.concatenate([part, jnp.zeros((tall - part.shape[0], SIDE), jnp.float32)], axis=0)
            total = total + pltpu.roll(jnp.where(keep, part, 0.0), (EDGE * g - origin) % SIDE, 1)
        out[...] = total


def unpack_side(packed, out):
    height = out.shape[0]
    tall = packed_rows(height)
    lane = iota((tall, SIDE), 1)
    right, left = packed[0:tall, :], packed[tall : 2 * tall, :]
    for g in range(TIERS):
        part = jnp.where(lane < EDGE, pltpu.roll(right, -EDGE * g % SIDE, 1), 0.0)
        part = part + jnp.where(lane >= SIDE - EDGE, pltpu.roll(left, (SIDE - EDGE - EDGE * g) % SIDE, 1), 0.0)
        top = g * tall
        count = min(tall, height - top)
        out[top : top + count, :] = part[0:count]


def own_kernel(rows, cols, scalars_in, own, guess, source, compact, scalars):
    fields = PARTS * rows
    scalars[...] = scalars_in[...]
    guess[...] = by_cells(own[0:fields, :], rows)
    source[...] = by_cells(own[fields : 2 * fields, :], rows)
    found = coefficients(*[own[2 * fields + k * rows : 2 * fields + (k + 1) * rows, :] for k in range(3)], scalars_in)
    for k in range(6):
        compact[k] = found[k]


def side_kernel(rows, cols, right, left, before, after, up, down, ends, sems):
    size = right.shape[0]
    copies = []
    for f in range(PARTS):
        copies.append(fetch(before.at[pl.ds((f + 1) * rows - 8, 8)], ends.at[0, f], sems.at[f]))
        copies.append(fetch(after.at[pl.ds(f * rows, 8)], ends.at[1, f], sems.at[PARTS + f]))
    for out in (up, down):
        out[0:size, :] = right[...]
        out[size : 2 * size, :] = left[...]
    for copy in copies:
        copy.wait()
    for out, p, row in ((up, 0, 7), (down, 1, 0)):
        far = jnp.concatenate([ends[p, f, row : row + 1, :] for f in range(PARTS)], axis=0)
        for t in range(cols // SIDE):
            out[2 * size + t * PARTS : 2 * size + (t + 1) * PARTS, :] = far[:, t * SIDE : (t + 1) * SIDE]


def first_kernel(
    rows, cols, scalars, own_guess, own_source, own_compact, before, after, own_side, before_side, after_side, kept, basis_out,
    compact_out, sums, sides, guess, basis, compact, spread, out_sems,
):
    lanes = cols + SIDE
    fields = PARTS * rows
    packed = (before_side, own_side, after_side)
    parts = []
    for p, main in enumerate((before, None, after)):
        unpack_side(packed[p], sides.at[p])
        parts += [(p, 0, main)] if main is not None else []
        parts += [(p, cols, sides.at[p])]
    here = pl.ds(rows, rows)
    guess[pl.ds(rows + 1, rows), :, 0:cols] = own_guess[...]
    basis[0, here, :, 0:cols] = own_source[...]
    compact[:, here, 0:cols] = own_compact[...]
    for p, at, ref in parts:
        size = ref.shape[1]
        guess[pl.ds(1 + p * rows, rows), :, at : at + size] = by_cells(ref[0:fields, :], rows)
        basis[0, pl.ds(p * rows, rows), :, at : at + size] = by_cells(ref[fields : 2 * fields, :], rows)
    shift, pair = [spread_scalar(scalars, i, (PARTS, lanes)) for i in (SHIFT, PAIR)]
    for p, at, ref in parts:
        size = ref.shape[1]
        level = [ref[2 * fields + k * rows : 2 * fields + (k + 1) * rows, :] for k in range(3)]
        found = coefficients(*level, scalars)
        for k in range(6):
            compact[k, p * rows : (p + 1) * rows, at : at + size] = found[k]
    spread_rows(compact, spread, 0, 3 * rows)
    end = before_side.shape[0] - cols // SIDE * PARTS
    for x, p in ((0, 0), (3 * rows + 1, 2)):
        for t in range(cols // SIDE):
            guess[x, :, t * SIDE : (t + 1) * SIDE] = packed[p][end + t * PARTS : end + (t + 1) * PARTS, :]
        guess[x, :, cols:lanes] = jnp.zeros((PARTS, SIDE), jnp.float32)
    half = rows // 2
    compact_out[...] = compact[:, half : half + 2 * rows, :]
    outs = []

    def start(base, count):
        made = []
        for i in range(count):
            x = base + i
            middle = guess[x + 1]
            applied = scaled_operator(middle, guess[x], guess[x + 2], [spread[k, x] for k in range(6)])
            made.append(basis[0, x] - applied * (1.0 / SCALE) - shift * middle)
        for i in range(count):
            basis[0, base + i] = made[i]

    by_groups(0, 3 * rows, start)
    for j in range(POWERS):
        next_block(basis, spread, j, pair * SCALE * SCALE)
        k = j + 1 - KEPT
        if k >= 0:
            outs.append(fetch(basis.at[j + 1, pl.ds(half, 2 * rows)], basis_out.at[k], out_sems.at[k]))
    kept[...] = basis[0:KEPT, half : half + 2 * rows]
    tile = packed_gram(basis, rows, rows, cols)
    for i in range(sums.shape[0]):
        sums[i] = tile
    for copy in outs:
        copy.wait()


def second_kernel(
    rows, cols, scalars, tiles, kept, basis_in, compact, guess, basis_out, solution, sums, old, basis, spread, weights, in_sems,
):
    shift, pair = scalars[SHIFT : SHIFT + 1, :], scalars[PAIR : PAIR + 1, :]
    copies = [fetch(basis_in.at[j], old.at[j], in_sems.at[j]) for j in range(BLOCKS - KEPT)]
    half = rows // 2
    spread_rows(compact, spread, 0, 2 * rows)
    update, residual = cycles(jnp.sum(tiles[...], axis=0), shift, pair)
    set_weights(weights, 0, residual)
    set_weights(weights, 1, update)
    for copy in copies:
        copy.wait()

    def block(j):
        return kept.at[j] if j < KEPT else old.at[j - KEPT]

    def one(t, _):
        for i in range(4):
            x = 4 * t + i
            basis[0, x] = mixed(weights, 0, [block(j)[x] for j in range(BLOCKS)])

    lax.fori_loop(0, 2 * rows // 4, one, None)

    def move(t, _):
        for i in range(4):
            x = 4 * t + i
            solution[x] = guess[x] + mixed(weights, 1, [block(j)[half + x, :, 0:cols] for j in range(POWERS)])

    lax.fori_loop(0, rows // 4, move, None)
    pair = spread_scalar(scalars, PAIR, basis.shape[2:])
    for j in range(POWERS):
        next_block(basis, spread, j, pair * SCALE * SCALE)
    basis_out[...] = basis[:, half : half + rows, :, 0:cols]
    tile = packed_gram(basis, half, rows, cols)
    for i in range(sums.shape[0]):
        sums[i] = tile


def third_kernel(rows, cols, scalars, tiles, old, start, solution, residual, made, turned, weights, sems):
    shift, pair = scalars[SHIFT : SHIFT + 1, :], scalars[PAIR : PAIR + 1, :]
    update, left = cycles(jnp.sum(tiles[...], axis=0), shift, pair)
    set_weights(weights, 0, left)
    set_weights(weights, 1, update)

    def move(t, _):
        for i in range(4):
            x = 4 * t + i
            blocks = [old[j, x] for j in range(BLOCKS)]
            made[0, x] = mixed(weights, 0, blocks)
            made[1, x] = start[x] + mixed(weights, 1, blocks[:POWERS])

    outs = []
    for half in range(2):
        count = rows // 2
        top = half * count
        lax.fori_loop(top // 4, (top + count) // 4, move, None)
        for k, out in enumerate((residual, solution)):
            turned[k, half] = jnp.swapaxes(made[k, top : top + count], 0, 1)
            outs.append(fetch(turned.at[k, half], out.at[:, pl.ds(top, count)], sems.at[k, half]))
    for copy in outs:
        copy.wait()


def summed(copies):
    got = lax.all_to_all(copies, "lat", 0, 0, tiled=True)
    near = jnp.sum(got, axis=0)
    sent = jnp.broadcast_to(near[None], (lax.axis_size("dep"),) + near.shape)
    return lax.all_to_all(sent, "dep", 0, 0, tiled=True)


def shards(x_start, source, eps_table, labels, pml_level):
    rows, cols = labels.shape
    lanes = cols + SIDE
    f32 = jnp.float32
    vmem = pl.BlockSpec(memory_space=pltpu.VMEM)
    anywhere = pl.BlockSpec(memory_space=pl.ANY)
    hbm = pl.BlockSpec(memory_space=pltpu.HBM)

    def params(mib):
        return pltpu.CompilerParams(vmem_limit_bytes=mib * MIB)

    lat_size = lax.axis_size("lat")
    start = x_start.reshape(PARTS * rows, cols)
    height = (2 * PARTS + 3) * rows
    count = PARTS * rows
    dma = pltpu.SemaphoreType.DMA
    tall = packed_rows(height)
    fields, first, last, scalars = pl.pallas_call(
        functools.partial(pack_kernel, rows, cols),
        out_shape=[
            jax.ShapeDtypeStruct((height, cols), f32),
            jax.ShapeDtypeStruct((tall, SIDE), f32),
            jax.ShapeDtypeStruct((tall, SIDE), f32),
            jax.ShapeDtypeStruct((3 * LABELS, SIDE), f32),
        ],
        in_specs=[hbm] * 5,
        out_specs=[vmem] * 4,
        scratch_shapes=[pltpu.SMEM(eps_table.shape, f32), pltpu.VMEM((3 * rows, cols), jnp.int32), dma((5,))],
        compiler_params=params(56),
        name="pack",
    )(eps_table, start, source.reshape(count, cols), labels, pml_level.reshape(2 * rows, cols))

    def along(array, axis, step):
        size = lax.axis_size(axis)
        return lax.ppermute(array, axis, [(i, i + step) for i in range(size) if 0 <= i + step < size])

    before, after = along(fields, "lat", 1), along(fields, "lat", -1)
    right, left = along(first, "dep", -1), along(last, "dep", 1)
    guess, seen, own_compact, scalars = pl.pallas_call(
        functools.partial(own_kernel, rows, cols),
        out_shape=[
            jax.ShapeDtypeStruct((rows, PARTS, cols), f32),
            jax.ShapeDtypeStruct((rows, PARTS, cols), f32),
            jax.ShapeDtypeStruct((6, rows, cols), f32),
            jax.ShapeDtypeStruct(scalars.shape, f32),
        ],
        in_specs=[vmem] * 2,
        out_specs=[vmem] * 4,
        compiler_params=params(8),
        name="own",
    )(scalars, fields)
    right, left, scalars = lax.optimization_barrier((right, left, scalars))
    both = 2 * tall + cols // SIDE * PARTS
    up, down = pl.pallas_call(
        functools.partial(side_kernel, rows, cols),
        out_shape=[jax.ShapeDtypeStruct((both, SIDE), f32)] * 2,
        in_specs=[vmem, vmem, anywhere, anywhere],
        out_specs=[vmem] * 2,
        scratch_shapes=[pltpu.VMEM((2, PARTS, 8, cols), f32), dma((2 * PARTS,))],
        compiler_params=params(4),
        name="side",
    )(right, left, before, after)
    before_side, after_side = along(up, "lat", 1), along(down, "lat", -1)

    kept, basis, compact, sums = pl.pallas_call(
        functools.partial(first_kernel, rows, cols),
        out_shape=[
            jax.ShapeDtypeStruct((KEPT, 2 * rows, PARTS, lanes), f32),
            jax.ShapeDtypeStruct((BLOCKS - KEPT, 2 * rows, PARTS, lanes), f32),
            jax.ShapeDtypeStruct((6, 2 * rows, lanes), f32),
            jax.ShapeDtypeStruct((lat_size, PARTS, SIDE), f32),
        ],
        in_specs=[vmem] * 9,
        out_specs=[vmem, hbm, vmem, vmem],
        scratch_shapes=[
            pltpu.VMEM((3, height, SIDE), f32),
            pltpu.VMEM((3 * rows + 2, PARTS, lanes), f32),
            pltpu.VMEM((BLOCKS, 3 * rows, PARTS, lanes), f32),
            pltpu.VMEM((6, 3 * rows, lanes), f32),
            pltpu.VMEM((6, 3 * rows, PARTS, lanes), f32),
            dma((BLOCKS,)),
        ],
        compiler_params=params(48),
        name="first",
    )(scalars, guess, seen, own_compact, before, after, up, before_side, after_side)
    tiles = summed(sums)
    basis, solution, sums = pl.pallas_call(
        functools.partial(second_kernel, rows, cols),
        out_shape=[
            jax.ShapeDtypeStruct((BLOCKS, rows, PARTS, cols), f32),
            jax.ShapeDtypeStruct((rows, PARTS, cols), f32),
            jax.ShapeDtypeStruct((lat_size, PARTS, SIDE), f32),
        ],
        in_specs=[vmem, vmem, vmem, hbm, vmem, vmem],
        out_specs=[vmem, vmem, vmem],
        scratch_shapes=[
            pltpu.VMEM((BLOCKS - KEPT, 2 * rows, PARTS, lanes), f32),
            pltpu.VMEM((BLOCKS, 2 * rows, PARTS, lanes), f32),
            pltpu.VMEM((6, 2 * rows, PARTS, lanes), f32),
            pltpu.VMEM((2, ANGLES, BLOCKS, PARTS, SIDE), f32),
            dma((BLOCKS,)),
        ],
        compiler_params=params(48),
        name="second",
    )(scalars, tiles, kept, basis, compact, guess)
    tiles = summed(sums)
    solution, residual = pl.pallas_call(
        functools.partial(third_kernel, rows, cols),
        out_shape=[jax.ShapeDtypeStruct((PARTS, rows, cols), f32)] * 2,
        in_specs=[vmem] * 4,
        out_specs=[hbm] * 2,
        scratch_shapes=[
            pltpu.VMEM((2, rows, PARTS, cols), f32),
            pltpu.VMEM((2, 2, PARTS, rows // 2, cols), f32),
            pltpu.VMEM((2, ANGLES, BLOCKS, PARTS, SIDE), f32),
            dma((2, 2)),
        ],
        compiler_params=params(8),
        name="third",
    )(scalars, tiles, basis, solution)
    return solution.reshape(x_start.shape), residual.reshape(x_start.shape)


def solution(mesh):
    in_specs = (
        P(None, None, "lat", "dep"),
        P(None, None, "lat", "dep"),
        P(),
        P("lat", "dep"),
        P(None, "lat", "dep"),
    )
    out_specs = (P(None, None, "lat", "dep"), P(None, None, "lat", "dep"))
    return jax.shard_map(shards, mesh=mesh, in_specs=in_specs, out_specs=out_specs, check_vma=False)
```
